256 devices in a mesh: grid: 2 (over y_lo), lat: 16 (over y_hi, x, core), lon: 8 (over z).
Axes of the slice: x: 4, y: 4 (y_hi: 2, y_lo: 2; y = y_hi * 2 + y_lo), z: 8, core: 2. Of those that a mesh axis runs over, the one named last changes fastest.
Arguments:
- fields: bfloat16 [2, 768, 128, 1024], P('grid', None, 'lat', 'lon'), may hold values from -6 to 6
- cotangent: bfloat16 [2, 768, 128, 1024], P('grid', None, 'lat', 'lon'), may hold values from -6 to 6
- wet_mask: int32 [128, 1024], P('lat', 'lon'), may hold values 0 or 1
- atmos_kernel: float32 [384, 49], replicated, may hold values from -0.875 to 0.875
- atmos_gain: float32 [384], replicated, may hold values from 0.5 to 1.5
- atmos_shift: float32 [384], replicated, may hold values from -3 to 3
- atmos_w_in: bfloat16 [384, 1536], replicated, may hold values from -0.3125 to 0.3125
- atmos_b_in: float32 [1536], replicated, may hold values from -3 to 3
- atmos_w_out: bfloat16 [1536, 384], replicated, may hold values from -0.15625 to 0.15625
- atmos_b_out: float32 [384], replicated, may hold values from -3 to 3
- atmos_scale: float32 [384], replicated, may hold values from 0.5 to 1.5
- ocean_kernel: float32 [256, 49], replicated, may hold values from -0.875 to 0.875
- ocean_gain: float32 [256], replicated, may hold values from 0.5 to 1.5
- ocean_shift: float32 [256], replicated, may hold values from -3 to 3
- ocean_w_in: bfloat16 [256, 1024], replicated, may hold values from -0.375 to 0.375
- ocean_b_in: float32 [1024], replicated, may hold values from -3 to 3
- ocean_w_out: bfloat16 [1024, 256], replicated, may hold values from -0.1875 to 0.1875
- ocean_b_out: float32 [256], replicated, may hold values from -3 to 3
- ocean_scale: float32 [256], replicated, may hold values from 0.5 to 1.5
- sources: int32 [2, 16, 8, 3], P('grid', 'lat', 'lon'), may hold values from 0 to 7, as said below
- regrid: bfloat16 [2, 16, 8, 3, 8, 128, 128], P('grid', 'lat', 'lon'), may hold values from -0.3125 to 0.3125
Outputs:
- advanced: bfloat16 [2, 768, 128, 1024], P('grid', None, 'lat', 'lon')
- field_grads: bfloat16 [2, 768, 128, 1024], P('grid', None, 'lat', 'lon')
The draws below stay inside these ranges and needn't reach their ends.
Inputs may be any that keep to these rules, and one draw needn't show every extreme that they name: `sources`: each tile lists 3 different tile columns of the other model in its own tile row.
All inputs are finite; a program needn't handle non-finite values. No bound on the sum of `wet_mask` on one device may be relied on, other than what follows from the above.
Results may differ from the reference program's by a relative error of at most 0.0049.
Values may be sent and summed in bfloat16 or wider, within the bound.
No kernel may reach another device: no remote copies, remote signals or barrier semaphores. Data moves between devices by JAX's collectives and lax.ppermute only.
A program may use at most 192 MiB of HBM per device.

```python
import math
import jax
import jax.numpy as jnp
from jax import lax

CA = 384
FA = 1536
CO = 256
FO = 1024
LA = 2
LO = 3
KF = 16
SLOTS = 3
ROWS_DEV = 8
COLS_DEV = 128
LC = 768
TLAT = 16
TLON = 8
NLAT = 128
NLON = 1024


def draw_sources(key, part):
    key = jax.random.fold_in(key, 11)
    scores = jax.random.randint(key, (2, TLAT, TLON, TLON), 0, 1 << 20, dtype=jnp.int32) * TLON + jnp.arange(TLON, dtype=jnp.int32)
    order = jnp.argsort(scores, axis=-1)
    return order[..., :SLOTS].astype(jnp.int32)


def with_ends(values, stream_key, least, high):
    spot = [jax.random.randint(jax.random.fold_in(stream_key, axis), (), 0, length) for axis, length in enumerate(values.shape)]
    longest = values.shape.index(max(values.shape))
    beside = spot[:longest] + [(spot[longest] + 1) % values.shape[longest]] + spot[longest + 1:]
    return values.at[tuple(spot)].set(least).at[tuple(beside)].set(high)


def shard_levels(rng, shape, pieces, smallest, high):
    def one(axis_at, blocks):
        heights = jax.random.uniform(jax.random.fold_in(jax.random.fold_in(rng, 6), axis_at), (blocks,), jnp.float32, smallest / len(pieces), high / len(pieces))
        return jnp.repeat(jnp.exp(heights), shape[axis_at] // blocks).reshape((-1,) + (1,) * (len(shape) - axis_at - 1))

    level = one(*pieces[0])
    for cut in pieces[1:]:
        level = level * one(*cut)
    return level


def normal_values(own_key, extent, deviation, most, pieces=(), held_as=jnp.bfloat16):
    entries = deviation * jax.random.normal(own_key, extent, jnp.float32)
    if pieces:
        entries = entries * shard_levels(own_key, extent, pieces, -0.22, 0.18)
    return jnp.clip(entries, -most, most).astype(held_as)


def setup_inputs(seed: int = 0) -> dict:
    arg_keys = jax.random.split(jax.random.key(seed), 22)
    return {
        "fields": normal_values(arg_keys[0], (2, LC, NLAT, NLON), 1.0, 6.0, ((0, 2), (2, 16), (3, 8))),
        "cotangent": normal_values(arg_keys[1], (2, LC, NLAT, NLON), 1.0, 6.0, ((0, 2), (2, 16), (3, 8))),
        "wet_mask": with_ends((jax.random.randint(arg_keys[2], (NLAT, NLON), 0, 10) < 7).astype(jnp.int32), jax.random.fold_in(arg_keys[2], 1), 0, 1),
        "atmos_kernel": normal_values(arg_keys[3], (CA, 49), 49 ** -0.5, 0.875, (), jnp.float32),
        "atmos_gain": jnp.clip(1.0 + 0.1 * jax.random.normal(arg_keys[4], (CA,), jnp.float32), 0.5, 1.5),
        "atmos_shift": normal_values(arg_keys[5], (CA,), 0.5, 3.0, (), jnp.float32),
        "atmos_w_in": normal_values(arg_keys[6], (CA, FA), CA ** -0.5, 0.3125),
        "atmos_b_in": normal_values(arg_keys[7], (FA,), 0.5, 3.0, (), jnp.float32),
        "atmos_w_out": normal_values(arg_keys[8], (FA, CA), FA ** -0.5, 0.15625),
        "atmos_b_out": normal_values(arg_keys[9], (CA,), 0.5, 3.0, (), jnp.float32),
        "atmos_scale": jnp.clip(jax.random.uniform(arg_keys[10], (CA,), jnp.float32, 0.5, 1.5), 0.5, 1.5),
        "ocean_kernel": normal_values(arg_keys[11], (CO, 49), 49 ** -0.5, 0.875, (), jnp.float32),
        "ocean_gain": jnp.clip(1.0 + 0.1 * jax.random.normal(arg_keys[12], (CO,), jnp.float32), 0.5, 1.5),
        "ocean_shift": normal_values(arg_keys[13], (CO,), 0.5, 3.0, (), jnp.float32),
        "ocean_w_in": normal_values(arg_keys[14], (CO, FO), CO ** -0.5, 0.375),
        "ocean_b_in": normal_values(arg_keys[15], (FO,), 0.5, 3.0, (), jnp.float32),
        "ocean_w_out": normal_values(arg_keys[16], (FO, CO), FO ** -0.5, 0.1875),
        "ocean_b_out": normal_values(arg_keys[17], (CO,), 0.5, 3.0, (), jnp.float32),
        "ocean_scale": jnp.clip(jax.random.uniform(arg_keys[18], (CO,), jnp.float32, 0.5, 1.5), 0.5, 1.5),
        "sources": draw_sources(jax.random.fold_in(arg_keys[21], 71), 0),
        "regrid": normal_values(arg_keys[20], (2, TLAT, TLON, SLOTS, ROWS_DEV, COLS_DEV, COLS_DEV), (SLOTS * COLS_DEV) ** -0.5, 0.3125, ((0, 2), (1, 16), (2, 8))),
    }


EPS = 1e-06
ROOT_TWO = math.sqrt(2.0)
NORMAL_PEAK = 1.0 / math.sqrt(2.0 * math.pi)
BEST = lax.Precision.HIGHEST

def gelu_value(hidden):
    return 0.5 * hidden * (1.0 + lax.erf(hidden / ROOT_TWO))

def gelu_slope(hidden):
    return 0.5 * (1.0 + lax.erf(hidden / ROOT_TWO)) + hidden * NORMAL_PEAK * jnp.exp(-0.5 * hidden * hidden)

def widen(field):
    padded = jnp.pad(field, ((0, 0), (3, 3), (0, 0)))
    return jnp.concatenate([padded[:, :, -3:], padded, padded[:, :, :3]], axis=2)

def depthwise(field, kernel_rows):
    lat_total, lon_total = (field.shape[1], field.shape[2])
    wide = widen(field)
    total = jnp.zeros(field.shape, jnp.float32)
    for row_off in range(7):
        for col_off in range(7):
            total = total + kernel_rows[:, row_off * 7 + col_off][:, None, None] * wide[:, row_off:row_off + lat_total, col_off:col_off + lon_total]
    return total

def depthwise_adjoint(grad, kernel_rows):
    lat_total, lon_total = (grad.shape[1], grad.shape[2])
    wide = widen(grad)
    total = jnp.zeros(grad.shape, jnp.float32)
    for row_off in range(7):
        for col_off in range(7):
            total = total + kernel_rows[:, row_off * 7 + col_off][:, None, None] * wide[:, 6 - row_off:6 - row_off + lat_total, 6 - col_off:6 - col_off + lon_total]
    return total

def to_tiles(field):
    return field.reshape(KF, TLAT, ROWS_DEV, TLON, COLS_DEV).transpose(1, 3, 0, 2, 4)

def from_tiles(tiles):
    return tiles.transpose(2, 0, 3, 1, 4).reshape(KF, TLAT * ROWS_DEV, TLON * COLS_DEV)

def remap(blocks, picks, source):
    tiles = to_tiles(source)
    row_index = jnp.arange(TLAT, dtype=jnp.int32)[:, None, None]
    picked = tiles[row_index, picks]
    mixed = jnp.einsum('ijphcd,ijpkhd->ijkhc', blocks.astype(jnp.float32), picked, precision=BEST)
    return from_tiles(mixed)

def remap_adjoint(blocks, picks, grad):
    tiles = to_tiles(grad)
    terms = jnp.einsum('ijphcd,ijkhc->ijpkhd', blocks.astype(jnp.float32), tiles, precision=BEST)
    onehot = (picks[..., None] == jnp.arange(TLON, dtype=jnp.int32)[None, None, None, :]).astype(jnp.float32)
    back = jnp.einsum('ijps,ijpkhd->iskhd', onehot, terms, precision=BEST)
    return from_tiles(back)

def cell_pass(mixed, out_cot, gain, shift, w_in, b_in, w_out, b_out, scale, chans):
    rows, lat_total, lon_total = mixed.shape
    levels = rows // chans
    cells = lat_total * lon_total
    width = math.gcd(cells, 2048)
    count = cells // width
    in_matrix = w_in.astype(jnp.float32)
    out_matrix = w_out.astype(jnp.float32)

    def arrange(field):
        return field.reshape(levels, chans, count, width).transpose(2, 0, 1, 3)

    def restore(field):
        return field.transpose(1, 2, 0, 3).reshape(rows, lat_total, lon_total)

    def one_block(pair):
        field, grad = pair
        centre = lax.optimization_barrier(jnp.mean(field, axis=1, keepdims=True))
        spread = field - centre
        inverse = lax.rsqrt(lax.optimization_barrier(jnp.mean(spread * spread, axis=1, keepdims=True)) + EPS)
        unit_field = spread * inverse
        normed = (unit_field * gain[None, :, None] + shift[None, :, None]).astype(jnp.bfloat16)
        hidden = jnp.einsum('cf,lcs->lfs', in_matrix, normed.astype(jnp.float32), precision=BEST) + b_in[None, :, None]
        active = gelu_value(hidden).astype(jnp.bfloat16)
        update = jnp.einsum('fc,lfs->lcs', out_matrix, active.astype(jnp.float32), precision=BEST) + b_out[None, :, None]
        up_grad = (scale[None, :, None] * grad).astype(jnp.bfloat16)
        active_grad = jnp.einsum('fc,lcs->lfs', out_matrix, up_grad.astype(jnp.float32), precision=BEST)
        hidden_grad = (active_grad * gelu_slope(hidden)).astype(jnp.bfloat16)
        normed_grad = jnp.einsum('cf,lfs->lcs', in_matrix, hidden_grad.astype(jnp.float32), precision=BEST)
        scaled = normed_grad * gain[None, :, None]
        inner = scaled - lax.optimization_barrier(jnp.mean(scaled, axis=1, keepdims=True)) - unit_field * lax.optimization_barrier(jnp.mean(scaled * unit_field, axis=1, keepdims=True))
        return (update, inverse * inner)
    update, mixed_grad = lax.map(one_block, (arrange(mixed), arrange(out_cot)))
    return (restore(update), restore(mixed_grad))

def reference(fields, cotangent, wet_mask, atmos_kernel, atmos_gain, atmos_shift, atmos_w_in, atmos_b_in, atmos_w_out, atmos_b_out, atmos_scale, ocean_kernel, ocean_gain, ocean_shift, ocean_w_in, ocean_b_in, ocean_w_out, ocean_b_out, ocean_scale, sources, regrid):
    wet = wet_mask.astype(jnp.float32)
    atm = fields[0].astype(jnp.float32)
    oce = fields[1].astype(jnp.float32) * wet[None]
    atm_cot = cotangent[0].astype(jnp.float32)
    oce_cot = cotangent[1].astype(jnp.float32) * wet[None]
    into_atm = remap(regrid[0], sources[0], oce[:KF])
    into_oce = remap(regrid[1], sources[1], atm[:KF])
    atm_rows = jnp.tile(atmos_kernel, (LA, 1))
    oce_rows = jnp.tile(ocean_kernel, (LO, 1))
    atm_mixed = depthwise(atm, atm_rows).at[:KF].add(into_atm)
    oce_mixed = depthwise(oce, oce_rows).at[:KF].add(into_oce)
    atm_update, atm_grad = cell_pass(atm_mixed, atm_cot, atmos_gain, atmos_shift, atmos_w_in, atmos_b_in, atmos_w_out, atmos_b_out, atmos_scale, CA)
    oce_update, oce_grad = cell_pass(oce_mixed, oce_cot, ocean_gain, ocean_shift, ocean_w_in, ocean_b_in, ocean_w_out, ocean_b_out, ocean_scale, CO)
    atm_out = atm + jnp.tile(atmos_scale, LA)[:, None, None] * atm_update
    oce_out = (oce + jnp.tile(ocean_scale, LO)[:, None, None] * oce_update) * wet[None]
    advanced = jnp.stack([atm_out, oce_out]).astype(jnp.bfloat16)
    atm_total = atm_cot + depthwise_adjoint(atm_grad, atm_rows)
    atm_total = atm_total.at[:KF].add(remap_adjoint(regrid[1], sources[1], oce_grad[:KF]))
    oce_total = oce_cot + depthwise_adjoint(oce_grad, oce_rows)
    oce_total = oce_total.at[:KF].add(remap_adjoint(regrid[0], sources[0], atm_grad[:KF]))
    oce_total = oce_total * wet[None]
    field_grads = jnp.stack([atm_total, oce_total]).astype(jnp.bfloat16)
    return (advanced, field_grads)
```

```python
import functools
import math

import jax
import jax.numpy as jnp
from jax import lax
from jax.experimental import pallas as pl
from jax.experimental.pallas import tpu as pltpu
from jax.sharding import PartitionSpec as P

KF = 16
EPS = 1e-06
INV_ROOT_TWO = 1.0 / math.sqrt(2.0)
NORMAL_PEAK = 1.0 / math.sqrt(2.0 * math.pi)
HALF_LOG2E = 0.5 * math.log2(math.e)
BF = jnp.bfloat16
F32 = jnp.float32
VMEM = pl.BlockSpec(memory_space=pltpu.VMEM)
SMEM = pl.BlockSpec(memory_space=pltpu.SMEM)
ANY = pl.BlockSpec(memory_space=pl.ANY)
STEPS = 8
ROWS = 8
LON = 128
TALL = 14


def params(**extra):
    return pltpu.CompilerParams(vmem_limit_bytes=56 * 2**20, **extra)


def cost(flops, nbytes):
    return pl.CostEstimate(flops=flops, bytes_accessed=nbytes, transcendentals=0)


def swap(block, axes, move):
    sizes = [lax.axis_size(axis) for axis in axes]
    route = []
    total = math.prod(sizes)
    for start in range(total):
        place = []
        rest = start
        for size in reversed(sizes):
            place.insert(0, rest % size)
            rest //= size
        goal = 0
        for size, value in zip(sizes, move(*place)):
            goal = goal * size + value
        route.append((start, goal))
    return lax.ppermute(block, axes, route)


def even_swap(block, axis):
    return swap(block, (axis,), lambda i: (i ^ 1,))


def odd_swap(block, axis):
    count = lax.axis_size(axis)
    return swap(block, (axis,), lambda i: ((((i + 1) ^ 1) - 1) % count,))


def model_keep(wet_ref):
    wet = wet_ref[...].astype(F32)
    return jnp.where(lax.axis_index("grid") == 1, wet, jnp.ones_like(wet))


def prepare_kernel(field_ref, wet_ref, rows_ref, even_ref, odd_ref, surface_ref, scratch):
    chans = field_ref.shape[0]
    keep = model_keep(wet_ref)
    held = field_ref[...].astype(F32) * keep[None]
    scratch[...] = held.reshape(chans * ROWS, LON)
    for row in range(ROWS):
        rows_ref[row] = scratch[pl.ds(row, chans, stride=ROWS), :].astype(BF)
    parity = lax.rem(lax.axis_index("lat"), 2)

    @pl.when(parity == 0)
    def _():
        even_ref[...] = rows_ref[ROWS - 3 :]
        odd_ref[...] = rows_ref[:3]

    @pl.when(parity == 1)
    def _():
        even_ref[...] = rows_ref[:3]
        odd_ref[...] = rows_ref[ROWS - 3 :]

    @pl.when(pl.program_id(0) == 0)
    def _():
        surface_ref[...] = rows_ref[:, :KF, :]


def prepare(field, wet_mask):
    stacked = field.shape[0]
    part = 256
    return pl.pallas_call(
        prepare_kernel,
        grid=(stacked // part,),
        in_specs=[
            pl.BlockSpec((part, ROWS, LON), lambda s: (s, 0, 0)),
            pl.BlockSpec((ROWS, LON), lambda s: (0, 0)),
        ],
        out_specs=[
            pl.BlockSpec((ROWS, part, LON), lambda s: (0, s, 0)),
            pl.BlockSpec((3, part, LON), lambda s: (0, s, 0)),
            pl.BlockSpec((3, part, LON), lambda s: (0, s, 0)),
            pl.BlockSpec((ROWS, KF, LON), lambda s: (0, 0, 0)),
        ],
        out_shape=[
            jax.ShapeDtypeStruct((ROWS, stacked, LON), BF),
            jax.ShapeDtypeStruct((3, stacked, LON), BF),
            jax.ShapeDtypeStruct((3, stacked, LON), BF),
            jax.ShapeDtypeStruct((ROWS, KF, LON), BF),
        ],
        scratch_shapes=[pltpu.VMEM((part * ROWS, LON), F32)],
        compiler_params=params(),
        cost_estimate=cost(10**6, 5 * 10**6),
        name="prepare",
    )(field, wet_mask)


def scaled_kernel(cot_ref, wet_ref, scale_ref, out_ref, scratch):
    chans = cot_ref.shape[0]
    keep = model_keep(wet_ref)
    held = cot_ref[...].astype(F32) * keep[None]
    scratch[...] = held.reshape(chans * ROWS, LON)
    scale = jnp.broadcast_to(scale_ref[...], (chans, LON))
    for row in range(ROWS):
        out_ref[row] = (scale * scratch[pl.ds(row, chans, stride=ROWS), :]).astype(BF)


def scaled_cotangent(cot, wet_mask, scale_rows):
    stacked = cot.shape[0]
    part = 256
    return pl.pallas_call(
        scaled_kernel,
        grid=(stacked // part,),
        in_specs=[
            pl.BlockSpec((part, ROWS, LON), lambda s: (s, 0, 0)),
            pl.BlockSpec((ROWS, LON), lambda s: (0, 0)),
            pl.BlockSpec((part, 1), lambda s: (s, 0)),
        ],
        out_specs=pl.BlockSpec((ROWS, part, LON), lambda s: (0, s, 0)),
        out_shape=jax.ShapeDtypeStruct((ROWS, stacked, LON), BF),
        scratch_shapes=[pltpu.VMEM((part * ROWS, LON), F32)],
        compiler_params=params(),
        cost_estimate=cost(10**6, 4 * 10**6),
        name="scaled_cotangent",
    )(cot, wet_mask, scale_rows)


def bands_kernel(taps_ref, out_ref):
    lane = lax.broadcasted_iota(jnp.int32, (8, LON), 1)
    chan = lax.broadcasted_iota(jnp.int32, (8, LON), 0)
    for block in range(3):
        for col in range(7):
            firsts = []
            for half in range(2):
                start = block * 16 + half * 8
                taps = taps_ref[0, col, start : start + 8, :]
                firsts.append(jnp.where(lax.rem(lane, 16) == chan + 8 * half, taps, 0.0))
            for row in range(ROWS):
                low = []
                high = []
                for first in firsts:
                    moved = pltpu.roll(first, 16 * row, 1) if row else first
                    low.append(jnp.where(lane >= 16 * row, moved, 0.0))
                    high.append(jnp.where(lane < 16 * row, moved, 0.0))
                place = slice(row * 16, row * 16 + 16)
                out_ref[0, 0, block, col, place, :LON] = jnp.concatenate(low, 0).astype(BF)
                out_ref[0, 0, block, col, place, LON:] = jnp.concatenate(high, 0).astype(BF)


def bands(taps):
    return pl.pallas_call(
        bands_kernel,
        grid=(2, STEPS),
        in_specs=[pl.BlockSpec((1, 7, 48, LON), lambda d, s: (d, 0, s, 0))],
        out_specs=pl.BlockSpec((1, 1, 3, 7, LON, 2 * LON), lambda d, s: (d, s, 0, 0, 0, 0)),
        out_shape=jax.ShapeDtypeStruct((2, STEPS, 3, 7, LON, 2 * LON), BF),
        compiler_params=params(),
        cost_estimate=cost(10**6, 25 * 10**6),
        name="bands",
    )(taps)


def gather_rows_kernel(own_ref, even_ref, odd_ref, tall_ref, packed_ref):
    lat = lax.axis_index("lat")
    first = lax.rem(lat, 2) == 0
    top_live = (lat > 0).astype(F32)
    bottom_live = (lat < lax.axis_size("lat") - 1).astype(F32)
    for row in range(3):
        even = even_ref[row].astype(F32)
        odd = odd_ref[row].astype(F32)
        tall_ref[row] = (jnp.where(first, odd, even) * top_live).astype(BF)
        tall_ref[ROWS + 3 + row] = (jnp.where(first, even, odd) * bottom_live).astype(BF)
    tall_ref[3 : ROWS + 3] = own_ref[...]
    lane = lax.broadcasted_iota(jnp.int32, (16, LON), 1)
    outer = (lane < 3) | (lane >= LON - 3)
    for row in range(TALL):
        total = jnp.zeros((16, LON), F32)
        for block in range(16):
            values = tall_ref[row, block * 16 : block * 16 + 16, :].astype(F32)
            values = jnp.where(outer, values, 0.0)
            total = total + (pltpu.roll(values, 8 * block, 1) if block else values)
        packed_ref[row] = total.astype(BF)


def gather_rows(own, even, odd):
    stacked = own.shape[1]
    return pl.pallas_call(
        gather_rows_kernel,
        grid=(stacked // 256,),
        in_specs=[
            pl.BlockSpec((ROWS, 256, LON), lambda s: (0, s, 0)),
            pl.BlockSpec((3, 256, LON), lambda s: (0, s, 0)),
            pl.BlockSpec((3, 256, LON), lambda s: (0, s, 0)),
        ],
        out_specs=[
            pl.BlockSpec((TALL, 256, LON), lambda s: (0, s, 0)),
            pl.BlockSpec((TALL, 16, LON), lambda s: (0, s, 0)),
        ],
        out_shape=[
            jax.ShapeDtypeStruct((TALL, stacked, LON), BF),
            jax.ShapeDtypeStruct((TALL, stacked // 16, LON), BF),
        ],
        compiler_params=params(),
        cost_estimate=cost(10**6, 5 * 10**6),
        name="gather_rows",
    )(own, even, odd)


def convolve(tall_ref, outer_ref, band_ref, block, starts):
    lane = lax.broadcasted_iota(jnp.int32, (16, LON), 1)
    inner = []
    beyond = []
    for start in starts:
        place = pl.multiple_of(start, 16)
        index = start // 16
        lot = pl.multiple_of((index // 16) * 16, 16)
        turn = lax.rem(LON - 8 * lax.rem(index, 16), LON)
        inner.append([tall_ref[row, pl.ds(place, 16), :] for row in range(TALL)])
        beyond.append(
            [
                pltpu.roll(outer_ref[row, pl.ds(lot, 16), :], turn, 1).astype(BF)
                for row in range(TALL)
            ]
        )
    blank = jnp.zeros((32, LON), BF)
    total = None
    for col in range(7):
        shift = col - 3
        sides = []
        for mine, other in zip(inner, beyond):
            if shift > 0:
                mine = [jnp.where(lane < shift, o, m) for m, o in zip(mine, other)]
            elif shift < 0:
                mine = [jnp.where(lane >= LON + shift, o, m) for m, o in zip(mine, other)]
            sides.append(jnp.concatenate(mine + [blank], axis=0))
        spread = jnp.concatenate(sides, axis=1)
        terms = jnp.dot(band_ref[0, 0, block, col], spread, preferred_element_type=F32)
        moved = []
        for level in range(len(starts)):
            piece = terms[:, level * LON : (level + 1) * LON]
            moved.append(pltpu.roll(piece, (-shift) % LON, 1) if shift else piece)
        total = moved if total is None else [t + m for t, m in zip(total, moved)]
    return total


def merge_outer(even_ref, odd_ref, outer_ref):
    first = lax.rem(lax.axis_index("lon"), 2) == 0
    lane = lax.broadcasted_iota(jnp.int32, even_ref.shape[1:], 1)
    from_right = lax.rem(lane, 8) < 4
    for row in range(TALL):
        even = even_ref[row].astype(F32)
        odd = odd_ref[row].astype(F32)
        right = jnp.where(first, even, odd)
        left = jnp.where(first, odd, even)
        outer_ref[row] = jnp.where(from_right, right, left)


def over_blocks(chans, levels, body):
    step = pl.program_id(0)
    count = chans // 16 // STEPS
    for block in range(count):
        base = (step * count + block) * 16
        body(block, [base + level * chans for level in range(levels)])


def mixing_kernel(models, tall_ref, even_ref, odd_ref, band_ref, out_ref, outer_ref):
    @pl.when(pl.program_id(0) == 0)
    def _():
        merge_outer(even_ref, odd_ref, outer_ref)

    def body(block, starts):
        totals = convolve(tall_ref, outer_ref, band_ref, block, starts)
        for start, total in zip(starts, totals):
            place = pl.ds(pl.multiple_of(start, 16), 16)
            for row in range(ROWS):
                out_ref[row, place, :] = total[row * 16 : row * 16 + 16]

    for which, (chans, levels) in enumerate(models):

        @pl.when(lax.axis_index("grid") == which)
        def _():
            over_blocks(chans, levels, body)


def mixing(models, tall, even, odd, band):
    stacked = tall.shape[1]

    return pl.pallas_call(
        functools.partial(mixing_kernel, models),
        grid=(STEPS,),
        in_specs=[
            VMEM,
            VMEM,
            VMEM,
            pl.BlockSpec((1, 1, 3, 7, LON, 2 * LON), lambda s: (0, s, 0, 0, 0, 0)),
        ],
        out_specs=pl.BlockSpec((ROWS, stacked, LON), lambda s: (0, 0, 0)),
        out_shape=jax.ShapeDtypeStruct((ROWS, stacked, LON), F32),
        scratch_shapes=[pltpu.VMEM((TALL, stacked // 16, LON), F32)],
        compiler_params=params(),
        cost_estimate=cost(3 * 10**9, 18 * 10**6),
        name="mixing",
    )(tall, even, odd, band)


def adjoint_kernel(
    models, tall_ref, even_ref, odd_ref, band_ref, cot_ref, wet_ref, coupling_ref, out_ref, outer_ref
):
    @pl.when(pl.program_id(0) == 0)
    def _():
        merge_outer(even_ref, odd_ref, outer_ref)

    keep = model_keep(wet_ref)

    def body(block, starts):
        totals = convolve(tall_ref, outer_ref, band_ref, block, starts)
        for level, (start, total) in enumerate(zip(starts, totals)):
            place = pl.ds(pl.multiple_of(start, 16), 16)
            shaped = total.reshape(ROWS, 16, LON)
            if level == 0:
                live = (start == 0).astype(F32)
                shaped = shaped + coupling_ref[...].astype(F32) * live
            by_chan = jnp.swapaxes(shaped, 0, 1)
            cot = cot_ref[place].astype(F32)
            out_ref[place] = ((cot + by_chan) * keep[None]).astype(BF)

    for which, (chans, levels) in enumerate(models):

        @pl.when(lax.axis_index("grid") == which)
        def _():
            over_blocks(chans, levels, body)


def adjoint(models, tall, even, odd, band, cot, wet_mask, coupling):

    stacked = tall.shape[1]
    return pl.pallas_call(
        functools.partial(adjoint_kernel, models),
        grid=(STEPS,),
        in_specs=[
            VMEM,
            VMEM,
            VMEM,
            pl.BlockSpec((1, 1, 3, 7, LON, 2 * LON), lambda s: (1, s, 0, 0, 0, 0)),
            VMEM,
            VMEM,
            VMEM,
        ],
        out_specs=pl.BlockSpec((stacked, ROWS, LON), lambda s: (0, 0, 0)),
        out_shape=jax.ShapeDtypeStruct((stacked, ROWS, LON), BF),
        scratch_shapes=[pltpu.VMEM((TALL, stacked // 16, LON), F32)],
        compiler_params=params(),
        cost_estimate=cost(3 * 10**9, 18 * 10**6),
        name="adjoint",
    )(tall, even, odd, band, cot, wet_mask, coupling)


def slot_of(source):
    apart = source ^ lax.axis_index("lon")
    return ((apart & 1) << 2) | (apart & 2) | ((apart >> 2) & 1)


def cells_kernel(
    models,
    mixed_ref,
    rows_ref,
    up_ref,
    wet_ref,
    sources_ref,
    regrid_ref,
    pieces_ref,
    *rest,
):
    weights = rest[:12]
    advanced_ref, grad_ref, even_ref, odd_ref, terms_ref = rest[12:17]
    forcing_ref, kept_ref, unit_ref, act_ref, back_ref, *held = rest[17:]
    sems = held[-1]
    held = held[:-1]

    slots = [slot_of(sources_ref[0, p]) for p in range(3)]
    for row in range(ROWS):
        total = None
        for p in range(3):
            part = lax.dot_general(
                pieces_ref[slots[p], row],
                regrid_ref[p, row],
                (((1,), (1,)), ((), ())),
                preferred_element_type=F32,
            )
            total = part if total is None else total + part
        forcing_ref[row] = total
    terms_ref[...] = jnp.zeros_like(terms_ref)

    def run(which, chans, levels):
        in_t, out_n, out_t, in_n, bias_in, table = weights[6 * which : 6 * which + 6]
        hidden_units = out_n.shape[0]
        in_t_v, out_n_v, out_t_v, in_n_v, bias_v, gain_v, shift_v, bias_out_v, scale_v = held[
            9 * which : 9 * which + 9
        ]
        copies = [
            pltpu.make_async_copy(src, dst, sems.at[4 * which + k])
            for k, (src, dst) in enumerate(
                ((in_t, in_t_v), (out_n, out_n_v), (out_t, out_t_v), (in_n, in_n_v))
            )
        ]
        for copy in copies:
            copy.start()
        bias_v[...] = jnp.broadcast_to(bias_in[...], bias_v.shape)
        for k, ref in enumerate((gain_v, shift_v, bias_out_v, scale_v)):
            ref[...] = jnp.broadcast_to(table[:, k : k + 1], ref.shape)
        for copy in copies:
            copy.wait()
        share = 1.0 / chans
        wide = 2 * LON
        part = 256

        def pair(values):
            return jnp.concatenate([values, values], axis=1)

        def chunk(index, carry):
            level = index // 4
            row = lax.rem(index, 4) * 2
            base = pl.multiple_of(level * chans, 16)
            place = pl.ds(base, chans)
            live = (level == 0).astype(F32)
            normed = []
            inverses = []
            for k in range(2):
                mixed = mixed_ref[row + k, place, :]
                top = mixed[:KF] + forcing_ref[row + k] * live
                mixed = jnp.concatenate([top, mixed[KF:]], axis=0)
                centre = jnp.sum(mixed, axis=0, keepdims=True) * share
                spread = mixed - centre
                inverse = lax.rsqrt(jnp.sum(spread * spread, axis=0, keepdims=True) * share + EPS)
                unit = spread * inverse
                unit_ref[k, :chans, :] = unit
                inverses.append(inverse)
                normed.append((unit * gain_v[...] + shift_v[...]).astype(BF))
            normed = jnp.concatenate(normed, axis=1)
            up = jnp.concatenate([up_ref[row, place, :], up_ref[row + 1, place, :]], axis=1)
            for start in range(0, hidden_units, part):
                these = slice(start, start + part)
                hidden = jnp.dot(in_t_v[these, :], normed, preferred_element_type=F32)
                active_grad = jnp.dot(out_n_v[these, :], up, preferred_element_type=F32)
                hidden = hidden + pair(bias_v[these, :])
                below = 0.5 + 0.5 * lax.erf(hidden * INV_ROOT_TWO)
                act_ref[these, :] = (hidden * below).astype(BF)
                bell = jnp.exp2((hidden * hidden) * -HALF_LOG2E) * NORMAL_PEAK
                back_ref[these, :] = (active_grad * (below + hidden * bell)).astype(BF)
            update = jnp.dot(
                out_t_v[...], act_ref[:hidden_units, :], preferred_element_type=F32
            )
            normed_grad = jnp.dot(
                in_n_v[...], back_ref[:hidden_units, :], preferred_element_type=F32
            )
            for k in range(2):
                lanes = slice(k * LON, (k + 1) * LON)
                moved = scale_v[...] * (update[:, lanes] + bias_out_v[...])
                kept_ref[row + k, place, :] = rows_ref[row + k, place, :].astype(F32) + moved
                scaled = normed_grad[:, lanes] * gain_v[...]
                unit = unit_ref[k, :chans, :]
                mean = jnp.sum(scaled, axis=0, keepdims=True) * share
                slope = jnp.sum(scaled * unit, axis=0, keepdims=True) * share
                grad = (inverses[k] * (scaled - mean - unit * slope)).astype(BF)
                grad_ref[row + k, place, :] = grad

                @pl.when(level == 0)
                def _():
                    for p in range(3):
                        terms_ref[slots[p], row + k] = jnp.dot(
                            grad[:KF], regrid_ref[p, row + k], preferred_element_type=F32
                        ).astype(BF)

            return carry

        lax.fori_loop(0, levels * 4, chunk, 0)

    for which, (chans, levels) in enumerate(models):

        @pl.when(lax.axis_index("grid") == which)
        def _():
            run(which, chans, levels)

    keep = model_keep(wet_ref)

    def finish(index, carry):
        place = pl.ds(pl.multiple_of(index * 16, 16), 16)
        by_chan = jnp.swapaxes(kept_ref[:, place, :], 0, 1)
        advanced_ref[place] = (by_chan * keep[None]).astype(BF)
        return carry

    lax.fori_loop(0, kept_ref.shape[1] // 16, finish, 0)
    parity = lax.rem(lax.axis_index("lat"), 2)

    @pl.when(parity == 0)
    def _():
        even_ref[...] = grad_ref[ROWS - 3 :]
        odd_ref[...] = grad_ref[:3]

    @pl.when(parity == 1)
    def _():
        even_ref[...] = grad_ref[:3]
        odd_ref[...] = grad_ref[ROWS - 3 :]


def cells(models, mixed, rows, up, wet_mask, sources, regrid, pieces, weights):

    stacked = rows.shape[1]
    held = []
    for which in range(2):
        in_t, out_n, out_t, in_n, bias_in, table = weights[6 * which : 6 * which + 6]
        held += [pltpu.VMEM(w.shape, BF) for w in (in_t, out_n, out_t, in_n)]
        held.append(pltpu.VMEM((bias_in.shape[0], LON), F32))
        held += [pltpu.VMEM((table.shape[0], LON), F32)] * 4
    most_chans = max(chans for chans, _ in models)
    most_units = max(weights[1].shape[0], weights[7].shape[0])
    return pl.pallas_call(
        functools.partial(cells_kernel, models),
        in_specs=[VMEM, VMEM, VMEM, VMEM, SMEM, VMEM, VMEM] + ([ANY] * 4 + [VMEM] * 2) * 2,
        out_specs=[VMEM] * 5,
        out_shape=[
            jax.ShapeDtypeStruct((stacked, ROWS, LON), BF),
            jax.ShapeDtypeStruct((ROWS, stacked, LON), BF),
            jax.ShapeDtypeStruct((3, stacked, LON), BF),
            jax.ShapeDtypeStruct((3, stacked, LON), BF),
            jax.ShapeDtypeStruct((8, ROWS, KF, LON), BF),
        ],
        scratch_shapes=[
            pltpu.VMEM((ROWS, KF, LON), F32),
            pltpu.VMEM((ROWS, stacked, LON), F32),
            pltpu.VMEM((2, most_chans, LON), F32),
            pltpu.VMEM((most_units, 2 * LON), BF),
            pltpu.VMEM((most_units, 2 * LON), BF),
        ]
        + held
        + [pltpu.SemaphoreType.DMA((8,))],
        compiler_params=params(),
        cost_estimate=cost(10**10, 20 * 10**6),
        name="cells",
    )(mixed, rows, up, wet_mask, sources, regrid, pieces, *weights)


def gather_surfaces(surface):
    block = swap(surface[None], ("grid",), lambda g: (1 - g,))
    for apart in (4, 2, 1):
        block = jnp.concatenate(
            [block, swap(block, ("lon",), lambda j, apart=apart: (j ^ apart,))], axis=0
        )
    return block


def scatter_terms(terms):
    for apart in (1, 2, 4):
        half = terms.shape[0] // 2
        came = swap(terms[half:], ("lon",), lambda j, apart=apart: (j ^ apart,))
        terms = (terms[:half].astype(F32) + came.astype(F32)).astype(BF)
    return swap(terms, ("grid",), lambda g: (1 - g,))[0]


def per_device(
    fields,
    cotangent,
    wet_mask,
    atmos_kernel,
    atmos_gain,
    atmos_shift,
    atmos_w_in,
    atmos_b_in,
    atmos_w_out,
    atmos_b_out,
    atmos_scale,
    ocean_kernel,
    ocean_gain,
    ocean_shift,
    ocean_w_in,
    ocean_b_in,
    ocean_w_out,
    ocean_b_out,
    ocean_scale,
    sources,
    regrid,
):
    stacked = fields.shape[1]
    models = tuple((w.shape[0], stacked // w.shape[0]) for w in (atmos_w_in, ocean_w_in))
    is_ocean = lax.axis_index("grid") == 1
    field, cot = fields[0], cotangent[0]
    rows, even, odd, surface = prepare(field, wet_mask)
    even = even_swap(even, "lat")
    odd = odd_swap(odd, "lat")
    pieces = gather_surfaces(surface)

    most, taken = atmos_kernel.shape
    by_step = ocean_kernel.reshape(STEPS, ocean_kernel.shape[0] // STEPS, taken)
    spare = most // STEPS - by_step.shape[1]
    ocean_steps = jnp.pad(by_step, ((0, 0), (0, spare), (0, 0))).reshape(most, taken)
    kernel = jnp.where(is_ocean, ocean_steps, atmos_kernel)
    both = jnp.stack([kernel, kernel[:, ::-1]]).reshape(2, most, 7, 7)
    both = jnp.pad(both.transpose(0, 3, 1, 2), ((0, 0), (0, 0), (0, 0), (0, 1)))
    taps = jnp.repeat(both, 16, axis=3)
    band = bands(taps)
    scale_rows = jnp.where(
        is_ocean,
        jnp.tile(ocean_scale, models[1][1]),
        jnp.tile(atmos_scale, models[0][1]),
    )
    up = scaled_cotangent(cot, wet_mask, scale_rows[:, None])
    weights = []
    for w_in, w_out, b_in, columns in (
        (atmos_w_in, atmos_w_out, atmos_b_in, (atmos_gain, atmos_shift, atmos_b_out, atmos_scale)),
        (ocean_w_in, ocean_w_out, ocean_b_in, (ocean_gain, ocean_shift, ocean_b_out, ocean_scale)),
    ):
        weights += [w_in.T, w_out, w_out.T, w_in, b_in[:, None], jnp.stack(columns, axis=1)]

    tall, packed = gather_rows(rows, even, odd)
    mixed = mixing(models, tall, even_swap(packed, "lon"), odd_swap(packed, "lon"), band)
    advanced, grad, even, odd, terms = cells(
        models, mixed, rows, up, wet_mask, sources[0, 0], regrid[0, 0, 0], pieces, weights
    )
    even = even_swap(even, "lat")
    odd = odd_swap(odd, "lat")
    coupling = scatter_terms(terms)
    tall, packed = gather_rows(grad, even, odd)
    field_grads = adjoint(
        models,
        tall,
        even_swap(packed, "lon"),
        odd_swap(packed, "lon"),
        band,
        cot,
        wet_mask,
        coupling,
    )
    return (advanced[None], field_grads[None])


def solution(mesh):
    placed = (
        (P("grid", None, "lat", "lon"),) * 2
        + (P("lat", "lon"),)
        + (P(),) * 16
        + (P("grid", "lat", "lon", None), P("grid", "lat", "lon", None, None, None, None))
    )
    return jax.shard_map(
        per_device,
        mesh=mesh,
        in_specs=placed,
        out_specs=(P("grid", None, "lat", "lon"), P("grid", None, "lat", "lon")),
        check_vma=False,
    )
```

```python
import functools
import math

import jax
import jax.numpy as jnp
from jax import lax
from jax.experimental import pallas as pl
from jax.experimental.pallas import tpu as pltpu
from jax.sharding import PartitionSpec as P

KF = 16
EPS = 1e-06
INV_ROOT_TWO = 1.0 / math.sqrt(2.0)
NORMAL_PEAK = 1.0 / math.sqrt(2.0 * math.pi)
HALF_LOG2E = 0.5 * math.log2(math.e)
BF = jnp.bfloat16
F32 = jnp.float32
VMEM = pl.BlockSpec(memory_space=pltpu.VMEM)
SMEM = pl.BlockSpec(memory_space=pltpu.SMEM)
ANY = pl.BlockSpec(memory_space=pl.ANY)
STEPS = 8
ROWS = 8
LON = 128
TALL = 14


def params(**extra):
    return pltpu.CompilerParams(vmem_limit_bytes=56 * 2**20, **extra)


def cost(flops, nbytes):
    return pl.CostEstimate(flops=flops, bytes_accessed=nbytes, transcendentals=0)


def swap(block, axes, move):
    sizes = [lax.axis_size(axis) for axis in axes]
    route = []
    total = math.prod(sizes)
    for start in range(total):
        place = []
        rest = start
        for size in reversed(sizes):
            place.insert(0, rest % size)
            rest //= size
        goal = 0
        for size, value in zip(sizes, move(*place)):
            goal = goal * size + value
        route.append((start, goal))
    return lax.ppermute(block, axes, route)


def even_swap(block, axis):
    return swap(block, (axis,), lambda i: (i ^ 1,))


def odd_swap(block, axis):
    count = lax.axis_size(axis)
    return swap(block, (axis,), lambda i: ((((i + 1) ^ 1) - 1) % count,))


def model_keep(wet_ref):
    wet = wet_ref[...].astype(F32)
    return jnp.where(lax.axis_index("grid") == 1, wet, jnp.ones_like(wet))


def pack_outer(rows_ref, packed_ref, lots, base=0):
    lane = lax.broadcasted_iota(jnp.int32, (16, LON), 1)
    outer = (lane < 3) | (lane >= LON - 3)
    for row in range(ROWS):
        for lot in range(lots):
            total = jnp.zeros((16, LON), F32)
            for block in range(16):
                start = (lot * 16 + block) * 16
                values = rows_ref[row, start : start + 16, :].astype(F32)
                values = jnp.where(outer, values, 0.0)
                total = total + (pltpu.roll(values, 8 * block, 1) if block else values)
            packed_ref[row, lot * 16 : lot * 16 + 16, :] = total.astype(BF)


def prepare_kernel(
    field_ref, wet_ref, rows_ref, even_ref, odd_ref, surface_ref, packed_ref, scratch
):
    chans = field_ref.shape[0]
    keep = model_keep(wet_ref)
    held = field_ref[...].astype(F32) * keep[None]
    scratch[...] = held.reshape(chans * ROWS, LON)
    for row in range(ROWS):
        rows_ref[row] = scratch[pl.ds(row, chans, stride=ROWS), :].astype(BF)
    parity = lax.rem(lax.axis_index("lat"), 2)

    @pl.when(parity == 0)
    def _():
        even_ref[...] = rows_ref[ROWS - 3 :]
        odd_ref[...] = rows_ref[:3]

    @pl.when(parity == 1)
    def _():
        even_ref[...] = rows_ref[:3]
        odd_ref[...] = rows_ref[ROWS - 3 :]

    @pl.when(pl.program_id(0) == 0)
    def _():
        surface_ref[...] = rows_ref[:, :KF, :]

    pack_outer(rows_ref, packed_ref, 1)


def prepare(field, wet_mask):
    stacked = field.shape[0]
    part = 256
    return pl.pallas_call(
        prepare_kernel,
        grid=(stacked // part,),
        in_specs=[
            pl.BlockSpec((part, ROWS, LON), lambda s: (s, 0, 0)),
            pl.BlockSpec((ROWS, LON), lambda s: (0, 0)),
        ],
        out_specs=[
            pl.BlockSpec((ROWS, part, LON), lambda s: (0, s, 0)),
            pl.BlockSpec((3, part, LON), lambda s: (0, s, 0)),
            pl.BlockSpec((3, part, LON), lambda s: (0, s, 0)),
            pl.BlockSpec((ROWS, KF, LON), lambda s: (0, 0, 0)),
            pl.BlockSpec((ROWS, 16, LON), lambda s: (0, s, 0)),
        ],
        out_shape=[
            jax.ShapeDtypeStruct((ROWS, stacked, LON), BF),
            jax.ShapeDtypeStruct((3, stacked, LON), BF),
            jax.ShapeDtypeStruct((3, stacked, LON), BF),
            jax.ShapeDtypeStruct((ROWS, KF, LON), BF),
            jax.ShapeDtypeStruct((ROWS, stacked // 16, LON), BF),
        ],
        scratch_shapes=[pltpu.VMEM((part * ROWS, LON), F32)],
        compiler_params=params(),
        cost_estimate=cost(10**6, 5 * 10**6),
        name="prepare",
    )(field, wet_mask)


def ready_kernel(models, row_ref, *refs):
    inputs, refs = refs[:6], refs[6:]
    in_t_ref, out_t_ref, bias_ref, table_ref, taps_ref = refs

    def run(first, chans, w_in, w_out, kernel):
        units = w_out.shape[0]
        in_t_ref[:units, :chans] = w_in[...].T
        out_t_ref[:chans, :units] = w_out[...].T

        def column(start):
            return jnp.broadcast_to(row_ref[0:1, start : start + LON], (LON, LON)).T

        for start in range(0, units, LON):
            bias_ref[start : start + LON, :] = column(first + start)
        for k in range(4):
            for start in range(0, chans, LON):
                table_ref[k, start : start + LON, :] = column(first + units + k * chans + start)
        taken = kernel.shape[0]
        tap = lax.broadcasted_iota(jnp.int32, (taken, LON), 0)
        group = lax.broadcasted_iota(jnp.int32, (taken, LON), 1) // 16
        by_chan = jnp.transpose(kernel[...]).astype(BF)
        for col in range(7):
            for flip in range(2):
                wanted = (6 - group) * 7 + (6 - col) if flip else group * 7 + col
                pick = ((tap == wanted) & (group < 7)).astype(F32).astype(BF)
                spread = jnp.dot(by_chan, pick, preferred_element_type=F32)
                taps_ref[flip, col, :chans, :] = spread.astype(BF)

    first = 0
    for which, (chans, _) in enumerate(models):
        w_in, w_out, kernel = inputs[3 * which : 3 * which + 3]

        @pl.when(lax.axis_index("grid") == which)
        def _():
            run(first, chans, w_in, w_out, kernel)

        first += w_out.shape[0] + 4 * chans


def ready(models, rows, arrays):
    most = max(chans for chans, _ in models)
    units = max(arrays[1].shape[0], arrays[4].shape[0])
    return pl.pallas_call(
        functools.partial(ready_kernel, models),
        in_specs=[VMEM] * 7,
        out_specs=[VMEM] * 5,
        out_shape=[
            jax.ShapeDtypeStruct((units, most), BF),
            jax.ShapeDtypeStruct((most, units), BF),
            jax.ShapeDtypeStruct((units, LON), F32),
            jax.ShapeDtypeStruct((4, most, LON), F32),
            jax.ShapeDtypeStruct((2, 7, most, LON), BF),
        ],
        compiler_params=params(),
        cost_estimate=cost(10**9, 10 * 10**6),
        name="ready",
    )(jnp.concatenate(rows)[None], *arrays)


def cotangent_kernel(cot_ref, wet_ref, scale_ref, out_ref, scratch):
    chans = cot_ref.shape[0]
    keep = model_keep(wet_ref)
    held = cot_ref[...].astype(F32) * keep[None]
    scratch[...] = held.reshape(chans * ROWS, LON)
    scale = jnp.concatenate(
        [
            jnp.broadcast_to(scale_ref[0, 0:1, start : start + LON], (LON, LON)).T
            for start in range(0, chans, LON)
        ],
        axis=0,
    )
    for row in range(ROWS):
        out_ref[row] = (scale * scratch[pl.ds(row, chans, stride=ROWS), :]).astype(BF)


def scaled_cotangent(cot, wet_mask, scale_rows):
    stacked = cot.shape[0]
    part = 256
    return pl.pallas_call(
        cotangent_kernel,
        grid=(stacked // part,),
        in_specs=[
            pl.BlockSpec((part, ROWS, LON), lambda s: (s, 0, 0)),
            pl.BlockSpec((ROWS, LON), lambda s: (0, 0)),
            pl.BlockSpec((1, 1, part), lambda s: (s, 0, 0)),
        ],
        out_specs=pl.BlockSpec((ROWS, part, LON), lambda s: (0, s, 0)),
        out_shape=jax.ShapeDtypeStruct((ROWS, stacked, LON), BF),
        scratch_shapes=[pltpu.VMEM((part * ROWS, LON), F32)],
        compiler_params=params(),
        cost_estimate=cost(10**6, 4 * 10**6),
        name="scaled_cotangent",
    )(cot, wet_mask, scale_rows.reshape(stacked // part, 1, part))


def build_taps(taps_ref, chan_start, band_ref, slot):
    lane = lax.broadcasted_iota(jnp.int32, (16, LON), 1)
    chan = lax.broadcasted_iota(jnp.int32, (16, LON), 0)
    for col in range(7):
        values = taps_ref[col, pl.ds(chan_start, 16), :].astype(F32)
        kept = jnp.where(lax.rem(lane, 16) == chan, values, 0.0)
        band_ref[slot, col * 16 : col * 16 + 16, :] = kept.astype(BF)


def convolve(rows_ref, halo_ref, outer_ref, band_ref, slot, starts):
    lane = lax.broadcasted_iota(jnp.int32, (16, LON), 1)
    inner = []
    beyond = []
    for start in starts:
        place = pl.ds(pl.multiple_of(start, 16), 16)
        index = start // 16
        lot = pl.ds(pl.multiple_of((index // 16) * 16, 16), 16)
        turn = lax.rem(LON - 8 * lax.rem(index, 16), LON)
        inner.append(
            [halo_ref[row, place, :] for row in range(3)]
            + [rows_ref[row, place, :] for row in range(ROWS)]
            + [halo_ref[row, place, :] for row in range(3, 6)]
        )
        beyond.append(
            [pltpu.roll(outer_ref[row, lot, :], turn, 1).astype(BF) for row in range(TALL)]
        )
    count = len(starts)
    blank = jnp.zeros((16, 2 * count * LON), BF)
    wide = [
        jnp.concatenate([side[row] for side in inner + beyond], axis=1) for row in range(TALL)
    ] + [blank]
    band = band_ref[slot]
    totals = [[] for _ in starts]
    for row in range(ROWS):
        spread = jnp.concatenate(wide[row : row + 8], axis=0)
        terms = jnp.dot(band, spread, preferred_element_type=F32)
        for level in range(count):
            total = None
            for col in range(7):
                shift = col - 3
                here = slice(col * 16, col * 16 + 16)
                piece = terms[here, level * LON : (level + 1) * LON]
                if shift:
                    other = terms[here, (count + level) * LON : (count + level + 1) * LON]
                    edge = lane < shift if shift > 0 else lane >= LON + shift
                    piece = pltpu.roll(jnp.where(edge, other, piece), (-shift) % LON, 1)
                total = piece if total is None else total + piece
            totals[level].append(total)
    return [jnp.concatenate(total, axis=0) for total in totals]


def convolve_all(chans, levels, taps_ref, rows_ref, halo_ref, outer_ref, band_ref, finish):
    count = chans // 16 // STEPS

    def step(index, carry):
        bases = [pl.multiple_of((index * count + block) * 16, 16) for block in range(count)]
        for block, base in enumerate(bases):
            build_taps(taps_ref, base, band_ref, block)
        for block, base in enumerate(bases):
            starts = [base + level * chans for level in range(levels)]
            for start, total in zip(
                starts, convolve(rows_ref, halo_ref, outer_ref, band_ref, block, starts)
            ):
                finish(start, total)
        return carry

    lax.fori_loop(0, STEPS, step, 0)


def merge_outer(outer_in, corner_even, corner_odd, outer_ref):
    first, top_live, bottom_live = lat_place()
    for row in range(3):
        even = corner_even[row].astype(F32)
        odd = corner_odd[row].astype(F32)
        outer_ref[row] = jnp.where(first, odd, even) * top_live
        outer_ref[ROWS + 3 + row] = jnp.where(first, even, odd) * bottom_live
    for row in range(ROWS):
        outer_ref[3 + row] = outer_in[row].astype(F32)


def lat_place():
    lat = lax.axis_index("lat")
    top = (lat > 0).astype(F32)
    bottom = (lat < lax.axis_size("lat") - 1).astype(F32)
    return lax.rem(lat, 2) == 0, top, bottom


def halo_copies(even_ref, odd_ref, halo_ref, sems):
    odd_lat = lax.rem(lax.axis_index("lat"), 2)
    return [
        pltpu.make_async_copy(even_ref, halo_ref.at[pl.ds(3 - 3 * odd_lat, 3)], sems.at[0]),
        pltpu.make_async_copy(odd_ref, halo_ref.at[pl.ds(3 * odd_lat, 3)], sems.at[1]),
    ]


def blank_beyond(halo_ref):
    lat = lax.axis_index("lat")

    @pl.when(lat == 0)
    def _():
        halo_ref[:3] = jnp.zeros_like(halo_ref[:3])

    @pl.when(lat == lax.axis_size("lat") - 1)
    def _():
        halo_ref[3:] = jnp.zeros_like(halo_ref[3:])


def adjoint_kernel(
    models,
    rows_hbm,
    even_hbm,
    odd_hbm,
    outer_in,
    corner_even,
    corner_odd,
    taps_hbm,
    cot_hbm,
    wet_ref,
    first_ref,
    out_ref,
    rows_ref,
    halo_ref,
    taps_ref,
    cot_ref,
    outer_ref,
    band_ref,
    sems,
):
    copies = [
        pltpu.make_async_copy(rows_hbm, rows_ref, sems.at[2]),
        pltpu.make_async_copy(taps_hbm.at[1], taps_ref, sems.at[3]),
        pltpu.make_async_copy(cot_hbm, cot_ref, sems.at[4]),
    ] + halo_copies(even_hbm, odd_hbm, halo_ref, sems)
    for copy in copies:
        copy.start()
    merge_outer(outer_in, corner_even, corner_odd, outer_ref)
    keep = model_keep(wet_ref)
    for copy in copies:
        copy.wait()
    blank_beyond(halo_ref)

    def finish(start, total):
        place = pl.ds(pl.multiple_of(start, 16), 16)
        by_chan = jnp.swapaxes(total.reshape(ROWS, 16, LON), 0, 1)
        whole = cot_ref[place].astype(F32) * keep[None] + by_chan
        out_ref[place] = (whole * keep[None]).astype(BF)
        first_ref[jnp.where(jnp.asarray(start == 0), 0, 1)] = whole

    for which, (chans, levels) in enumerate(models):

        @pl.when(lax.axis_index("grid") == which)
        def _():
            convolve_all(
                chans, levels, taps_ref, rows_ref, halo_ref, outer_ref, band_ref, finish
            )


def conv_scratch(stacked, most):
    return [
        pltpu.VMEM((ROWS, stacked, LON), BF),
        pltpu.VMEM((6, stacked, LON), BF),
        pltpu.VMEM((7, most, LON), BF),
    ]


def adjoint(models, rows, even, odd, outer, corner_even, corner_odd, taps, cot, wet_mask):
    stacked = rows.shape[1]
    most = taps.shape[2]
    return pl.pallas_call(
        functools.partial(adjoint_kernel, models),
        in_specs=[ANY] * 3 + [VMEM] * 3 + [ANY] * 2 + [VMEM],
        out_specs=[VMEM, VMEM],
        out_shape=[
            jax.ShapeDtypeStruct((2, KF, ROWS, LON), F32),
            jax.ShapeDtypeStruct((stacked, ROWS, LON), BF),
        ],
        scratch_shapes=conv_scratch(stacked, most)
        + [
            pltpu.VMEM((stacked, ROWS, LON), BF),
            pltpu.VMEM((TALL, stacked // 16, LON), F32),
            pltpu.VMEM((3, 112, LON), BF),
            pltpu.SemaphoreType.DMA((5,)),
        ],
        compiler_params=params(),
        cost_estimate=cost(3 * 10**9, 8 * 10**6),
        name="adjoint",
    )(rows, even, odd, outer, corner_even, corner_odd, taps, cot, wet_mask)


def couple_kernel(first_ref, near_ref, far_ref, wet_ref, _, out_hbm, held_ref, sem):
    both = near_ref[...].astype(F32) + far_ref[...].astype(F32)
    keep = model_keep(wet_ref)
    held_ref[...] = ((first_ref[0] + jnp.swapaxes(both, 0, 1)) * keep[None]).astype(BF)
    copy = pltpu.make_async_copy(held_ref, out_hbm.at[pl.ds(0, KF)], sem)
    copy.start()
    copy.wait()


def couple(first, near, far, wet_mask, grads):
    return pl.pallas_call(
        couple_kernel,
        in_specs=[VMEM] * 4 + [ANY],
        out_specs=ANY,
        out_shape=jax.ShapeDtypeStruct(grads.shape, BF),
        input_output_aliases={4: 0},
        scratch_shapes=[pltpu.VMEM((KF, ROWS, LON), BF), pltpu.SemaphoreType.DMA],
        compiler_params=params(),
        cost_estimate=cost(10**5, 10**6),
        name="couple",
    )(first, near, far, wet_mask, grads)


def advance_kernel(rows_ref, wet_ref, out_ref):
    keep = model_keep(wet_ref)

    def turn(index, carry):
        place = pl.ds(pl.multiple_of(index * 16, 16), 16)
        by_chan = jnp.swapaxes(rows_ref[:, place, :].astype(F32), 0, 1)
        out_ref[place] = (by_chan * keep[None]).astype(BF)
        return carry

    lax.fori_loop(0, rows_ref.shape[1] // 16, turn, 0)


def advance(rows, wet_mask):
    stacked = rows.shape[1]
    part = 256
    return pl.pallas_call(
        advance_kernel,
        grid=(stacked // part,),
        in_specs=[
            pl.BlockSpec((ROWS, part, LON), lambda s: (0, s, 0)),
            pl.BlockSpec((ROWS, LON), lambda s: (0, 0)),
        ],
        out_specs=pl.BlockSpec((part, ROWS, LON), lambda s: (s, 0, 0)),
        out_shape=jax.ShapeDtypeStruct((stacked, ROWS, LON), BF),
        compiler_params=params(),
        cost_estimate=cost(10**6, 4 * 10**6),
        name="advance",
    )(rows, wet_mask)


def slot_of(source):
    apart = source ^ lax.axis_index("lon")
    far = apart >> 2
    return far | ((((apart >> 1) ^ far) & 1) << 1) | (((apart ^ far) & 1) << 2)


def cells_kernel(models, *refs):
    (
        rows_hbm,
        even_hbm,
        odd_hbm,
        outer_in,
        corner_even,
        corner_odd,
        taps_hbm,
        up_hbm,
        wet_ref,
        sources_ref,
        regrid_hbm,
        *refs,
    ) = refs
    pieces_hbm, refs = refs[:4], refs[4:]
    weights, refs = refs[:8], refs[8:]
    (advanced_hbm, grad_hbm, even_out, odd_out, packed_ref, *terms), refs = refs[:7], refs[7:]
    rows_ref, halo_ref, taps_ref, up_ref, regrid_ref, pieces_ref, outer_ref, band_ref = refs[:8]
    mixed_ref, forcing_ref, advanced_ref, grad_ref = refs[8:12]
    kept, refs = (refs[12:16], refs[16:20]), refs[20:]
    in_t_v, out_n_v, out_t_v, in_n_v, bias_v, table_v, sems, weight_sems = refs
    early = halo_copies(even_hbm, odd_hbm, halo_ref, sems) + [
        pltpu.make_async_copy(rows_hbm, rows_ref, sems.at[2]),
        pltpu.make_async_copy(taps_hbm.at[0], taps_ref, sems.at[3]),
    ]
    late = [
        pltpu.make_async_copy(src, dst, sems.at[4 + k])
        for k, (src, dst) in enumerate(
            [(up_hbm, up_ref), (regrid_hbm, regrid_ref)]
            + [
                (piece, pieces_ref.at[pl.ds(start, piece.shape[0])])
                for piece, start in zip(pieces_hbm, (0, 1, 2, 4))
            ]
        )
    ]
    for copy in early:
        copy.start()
    for copy in late:
        copy.start()
    merge_outer(outer_in, corner_even, corner_odd, outer_ref)
    for copy in early:
        copy.wait()
    blank_beyond(halo_ref)

    def mix(chans, levels):
        def finish(start, total):
            place = pl.ds(pl.multiple_of(start, 16), 16)
            for row in range(ROWS):
                mixed_ref[row, place, :] = total[row * 16 : row * 16 + 16]

        convolve_all(chans, levels, taps_ref, rows_ref, halo_ref, outer_ref, band_ref, finish)

    def force():
        for copy in late:
            copy.wait()
        slots = [slot_of(sources_ref[0, p]) for p in range(3)]
        for row in range(ROWS):
            total = None
            for p in range(3):
                part = lax.dot_general(
                    pieces_ref[slots[p], row],
                    regrid_ref[p, row],
                    (((1,), (1,)), ((), ())),
                    preferred_element_type=F32,
                )
                total = part if total is None else total + part
            forcing_ref[row] = total
        for ref in terms:
            ref[...] = jnp.zeros_like(ref)
        return slots

    def run(which, chans, levels):
        in_t, out_t, bias, table = weights[4:]
        in_n, out_n = weights[2 * which : 2 * which + 2]
        hidden_units = out_n.shape[0]
        units, wide_chans = pl.ds(0, hidden_units), pl.ds(0, chans)
        in_t_w, out_n_w = in_t_v.at[units, wide_chans], out_n_v.at[units, wide_chans]
        out_t_w, in_n_w = out_t_v.at[wide_chans, units], in_n_v.at[wide_chans, units]
        copies = [
            pltpu.make_async_copy(src, dst, weight_sems.at[k])
            for k, (src, dst) in enumerate(
                (
                    (in_t.at[units, wide_chans], in_t_w),
                    (out_n, out_n_w),
                    (out_t.at[wide_chans, units], out_t_w),
                    (in_n, in_n_w),
                    (bias, bias_v),
                    (table, table_v),
                )
            )
        ]
        for copy in copies:
            copy.start()
        gain_v, shift_v, bias_out_v, scale_v = [table_v.at[k, wide_chans] for k in range(4)]
        mix(chans, levels)
        slots = force()
        for copy in copies:
            copy.wait()
        share = 1.0 / chans
        wide = 2 * LON
        part = 256

        def pair(values):
            return jnp.concatenate([values, values], axis=1)

        def place_of(index):
            return lax.rem(index, 4) * 2, pl.ds(pl.multiple_of(index // 4 * chans, 16), chans)

        def front(index, slot):
            row, place = place_of(index)
            live = jnp.asarray(index < 4).astype(F32)
            act_ref, back_ref, unit_ref, inverse_ref = kept[slot]
            normed = []
            for k in range(2):
                mixed = mixed_ref[row + k, place, :]
                top = mixed[:KF] + forcing_ref[row + k] * live
                mixed = jnp.concatenate([top, mixed[KF:]], axis=0)
                centre = jnp.sum(mixed, axis=0, keepdims=True) * share
                spread = mixed - centre
                inverse = lax.rsqrt(jnp.sum(spread * spread, axis=0, keepdims=True) * share + EPS)
                unit = spread * inverse
                unit_ref[k, :chans, :] = unit
                inverse_ref[k] = jnp.broadcast_to(inverse, (8, LON))
                normed.append((unit * gain_v[...] + shift_v[...]).astype(BF))
            normed = jnp.concatenate(normed, axis=1)
            up = jnp.concatenate([up_ref[row, place, :], up_ref[row + 1, place, :]], axis=1)
            for start in range(0, hidden_units, part):
                these = slice(start, start + part)
                hidden = jnp.dot(in_t_w[these, :], normed, preferred_element_type=F32)
                active_grad = jnp.dot(out_n_w[these, :], up, preferred_element_type=F32)
                hidden = hidden + pair(bias_v[these, :])
                below = 0.5 + 0.5 * lax.erf(hidden * INV_ROOT_TWO)
                act_ref[these, :] = (hidden * below).astype(BF)
                bell = jnp.exp2((hidden * hidden) * -HALF_LOG2E) * NORMAL_PEAK
                back_ref[these, :] = (active_grad * (below + hidden * bell)).astype(BF)

        def back(index, slot):
            row, place = place_of(index)
            act_ref, back_ref, unit_ref, inverse_ref = kept[slot]
            update = jnp.dot(
                out_t_w[...], act_ref[:hidden_units, :], preferred_element_type=F32
            )
            normed_grad = jnp.dot(
                in_n_w[...], back_ref[:hidden_units, :], preferred_element_type=F32
            )
            for k in range(2):
                lanes = slice(k * LON, (k + 1) * LON)
                moved = scale_v[...] * (update[:, lanes] + bias_out_v[...])
                total = rows_ref[row + k, place, :].astype(F32) + moved
                advanced_ref[row + k, place, :] = total.astype(BF)
                scaled = normed_grad[:, lanes] * gain_v[...]
                unit = unit_ref[k, :chans, :]
                mean = jnp.sum(scaled, axis=0, keepdims=True) * share
                slope = jnp.sum(scaled * unit, axis=0, keepdims=True) * share
                inverse = inverse_ref[k, 0:1, :]
                grad_ref[row + k, place, :] = (inverse * (scaled - mean - unit * slope)).astype(BF)

        count = levels * 4
        front(0, 0)

        def turn(index, carry):
            front(2 * index + 1, 1)
            back(2 * index, 0)
            front(2 * index + 2, 0)
            back(2 * index + 1, 1)
            return carry

        lax.fori_loop(0, count // 2 - 1, turn, 0)
        front(count - 1, 1)
        back(count - 2, 0)
        back(count - 1, 1)
        for row in range(ROWS):
            for p in range(3):
                term = jnp.dot(
                    grad_ref[row, :KF, :], regrid_ref[p, row], preferred_element_type=F32
                ).astype(BF)
                for side, ref in enumerate(terms):

                    @pl.when(slots[p] // 4 == side)
                    def _():
                        ref[lax.rem(slots[p], 4), row] = term

    for which, (chans, levels) in enumerate(models):

        @pl.when(lax.axis_index("grid") == which)
        def _():
            run(which, chans, levels)

    odd_lat = lax.rem(lax.axis_index("lat"), 2)
    lower = ROWS - 3
    leaving = [
        pltpu.make_async_copy(grad_ref.at[pl.ds(lower * (1 - odd_lat), 3)], even_out, sems.at[0]),
        pltpu.make_async_copy(grad_ref.at[pl.ds(lower * odd_lat, 3)], odd_out, sems.at[1]),
        pltpu.make_async_copy(grad_ref, grad_hbm, sems.at[2]),
        pltpu.make_async_copy(advanced_ref, advanced_hbm, sems.at[3]),
    ]
    for copy in leaving:
        copy.start()
    pack_outer(grad_ref, packed_ref, grad_ref.shape[1] // 256)
    for copy in leaving:
        copy.wait()


def cells(
    models,
    rows,
    even,
    odd,
    outer,
    corner_even,
    corner_odd,
    taps,
    up,
    wet_mask,
    sources,
    regrid,
    pieces,
    weights,
):
    stacked = rows.shape[1]
    most_chans = max(chans for chans, _ in models)
    most_units = weights[4].shape[0]
    return pl.pallas_call(
        functools.partial(cells_kernel, models),
        in_specs=[ANY] * 3
        + [VMEM] * 3
        + [ANY] * 2
        + [VMEM, SMEM]
        + [ANY] * (1 + 4 + 8),
        out_specs=[ANY] * 4 + [VMEM] * 3,
        out_shape=[
            jax.ShapeDtypeStruct((ROWS, stacked, LON), BF),
            jax.ShapeDtypeStruct((ROWS, stacked, LON), BF),
            jax.ShapeDtypeStruct((3, stacked, LON), BF),
            jax.ShapeDtypeStruct((3, stacked, LON), BF),
            jax.ShapeDtypeStruct((ROWS, stacked // 16, LON), BF),
            jax.ShapeDtypeStruct((4, ROWS, KF, LON), BF),
            jax.ShapeDtypeStruct((4, ROWS, KF, LON), BF),
        ],
        scratch_shapes=conv_scratch(stacked, taps.shape[2])
        + [
            pltpu.VMEM(up.shape, BF),
            pltpu.VMEM(regrid.shape, BF),
            pltpu.VMEM((8, ROWS, KF, LON), BF),
            pltpu.VMEM((TALL, stacked // 16, LON), F32),
            pltpu.VMEM((3, 112, LON), BF),
            pltpu.VMEM((ROWS, stacked, LON), F32),
            pltpu.VMEM((ROWS, KF, LON), F32),
            pltpu.VMEM((ROWS, stacked, LON), BF),
            pltpu.VMEM((ROWS, stacked, LON), BF),
        ]
        + [
            pltpu.VMEM((most_units, 2 * LON), BF),
            pltpu.VMEM((most_units, 2 * LON), BF),
            pltpu.VMEM((2, most_chans, LON), F32),
            pltpu.VMEM((2, 8, LON), F32),
        ]
        * 2
        + [
            pltpu.VMEM((most_units, most_chans), BF),
            pltpu.VMEM((most_units, most_chans), BF),
            pltpu.VMEM((most_chans, most_units), BF),
            pltpu.VMEM((most_chans, most_units), BF),
            pltpu.VMEM((most_units, LON), F32),
            pltpu.VMEM((4, most_chans, LON), F32),
            pltpu.SemaphoreType.DMA((10,)),
            pltpu.SemaphoreType.DMA((6,)),
        ],
        compiler_params=params(),
        cost_estimate=cost(10**10, 20 * 10**6),
        name="cells",
    )(
        rows,
        even,
        odd,
        outer,
        corner_even,
        corner_odd,
        taps,
        up,
        wet_mask,
        sources,
        regrid,
        *pieces,
        *weights,
    )


def swap_outer(packed):
    first = lax.rem(lax.axis_index("lon"), 2) == 0
    east_west = [even_swap(packed, "lon"), odd_swap(packed, "lon")]
    lane = lax.broadcasted_iota(jnp.int32, packed.shape, 2)
    from_even = (lax.rem(lane, 8) < 4) == first
    outer = jnp.where(from_even, *east_west)
    north = lax.rem(lax.axis_index("lat"), 2) == 1
    ends = (outer[:3], outer[ROWS - 3 :])
    even = even_swap(jnp.where(north, ends[0], ends[1]), "lat")
    odd = odd_swap(jnp.where(north, ends[1], ends[0]), "lat")
    return outer, even, odd


def cross(block, apart):
    return swap(block, ("grid", "lon"), lambda g, j: (1 - g, j ^ apart))


def lon_swap(block, apart):
    return swap(block, ("lon",), lambda j: (j ^ apart,))


def per_device(
    fields,
    cotangent,
    wet_mask,
    atmos_kernel,
    atmos_gain,
    atmos_shift,
    atmos_w_in,
    atmos_b_in,
    atmos_w_out,
    atmos_b_out,
    atmos_scale,
    ocean_kernel,
    ocean_gain,
    ocean_shift,
    ocean_w_in,
    ocean_b_in,
    ocean_w_out,
    ocean_b_out,
    ocean_scale,
    sources,
    regrid,
):
    stacked = fields.shape[1]
    models = tuple((w.shape[0], stacked // w.shape[0]) for w in (atmos_w_in, ocean_w_in))
    is_ocean = lax.axis_index("grid") == 1
    field, cot = fields[0], cotangent[0]
    rows, even, odd, surface, packed = prepare(field, wet_mask)
    pieces = [cross(surface[None], 0), cross(surface[None], 7)]
    around = swap_outer(packed)
    even = even_swap(even, "lat")
    odd = odd_swap(odd, "lat")
    scale_rows = jnp.where(
        is_ocean,
        jnp.tile(ocean_scale, models[1][1]),
        jnp.tile(atmos_scale, models[0][1]),
    )
    up = scaled_cotangent(cot, wet_mask, scale_rows[:, None])
    pieces.append(lon_swap(jnp.concatenate(pieces, axis=0), 2))
    *pieces, up = lax.optimization_barrier((*pieces, up))
    pieces.append(lon_swap(jnp.concatenate(pieces, axis=0), 1))
    made = ready(
        models,
        (
            atmos_b_in,
            atmos_gain,
            atmos_shift,
            atmos_b_out,
            atmos_scale,
            ocean_b_in,
            ocean_gain,
            ocean_shift,
            ocean_b_out,
            ocean_scale,
        ),
        (
            atmos_w_in,
            atmos_w_out,
            atmos_kernel.T,
            ocean_w_in,
            ocean_w_out,
            ocean_kernel.T,
        ),
    )
    around, pieces, made = lax.optimization_barrier((around, pieces, made))
    in_t, out_t, bias, table, taps = made
    weights = [atmos_w_in, atmos_w_out, ocean_w_in, ocean_w_out, in_t, out_t, bias, table]
    advanced, grad, even, odd, packed, near, far = cells(
        models,
        rows,
        even,
        odd,
        *around,
        taps,
        up,
        wet_mask,
        sources[0, 0],
        regrid[0, 0, 0],
        pieces,
        weights,
    )
    came = lon_swap(far, 1)
    around = swap_outer(packed)
    even = even_swap(even, "lat")
    odd = odd_swap(odd, "lat")
    sums = [(near[k : k + 2].astype(F32) + came[k : k + 2].astype(F32)) for k in (0, 2)]
    came = lon_swap(sums[1].astype(BF), 2)
    advanced = advance(advanced, wet_mask)
    came, advanced = lax.optimization_barrier((came, advanced))
    ends = [(sums[0][k] + came[k].astype(F32)).astype(BF) for k in range(2)]
    coupling = cross(ends[0], 0), cross(ends[1], 7)
    first, field_grads = adjoint(models, grad, even, odd, *around, taps, cot, wet_mask)
    field_grads = couple(first, *coupling, wet_mask, field_grads)
    return (advanced[None], field_grads[None])


def solution(mesh):
    placed = (
        (P("grid", None, "lat", "lon"),) * 2
        + (P("lat", "lon"),)
        + (P(),) * 16
        + (P("grid", "lat", "lon", None), P("grid", "lat", "lon", None, None, None, None))
    )
    return jax.shard_map(
        per_device,
        mesh=mesh,
        in_specs=placed,
        out_specs=(P("grid", None, "lat", "lon"), P("grid", None, "lat", "lon")),
        check_vma=False,
    )
```

```python
import functools
import math

import jax
import jax.numpy as jnp
from jax import lax
from jax.experimental import pallas as pl
from jax.experimental.pallas import tpu as pltpu
from jax.sharding import PartitionSpec as P

KF = 16
EPS = 1e-06
INV_ROOT_TWO = 1.0 / math.sqrt(2.0)
NORMAL_PEAK = 1.0 / math.sqrt(2.0 * math.pi)
HALF_LOG2E = 0.5 * math.log2(math.e)
BF = jnp.bfloat16
F32 = jnp.float32
VMEM = pl.BlockSpec(memory_space=pltpu.VMEM)
SMEM = pl.BlockSpec(memory_space=pltpu.SMEM)
ANY = pl.BlockSpec(memory_space=pl.ANY)
STEPS = 8
ROWS = 8
LON = 128
TALL = 14


def params(**extra):
    return pltpu.CompilerParams(vmem_limit_bytes=56 * 2**20, **extra)


def cost(flops, nbytes):
    return pl.CostEstimate(flops=flops, bytes_accessed=nbytes, transcendentals=0)


def swap(block, axes, move):
    sizes = [lax.axis_size(axis) for axis in axes]
    route = []
    total = math.prod(sizes)
    for start in range(total):
        place = []
        rest = start
        for size in reversed(sizes):
            place.insert(0, rest % size)
            rest //= size
        goal = 0
        for size, value in zip(sizes, move(*place)):
            goal = goal * size + value
        route.append((start, goal))
    return lax.ppermute(block, axes, route)


def even_swap(block, axis):
    return swap(block, (axis,), lambda i: (i ^ 1,))


def odd_swap(block, axis):
    count = lax.axis_size(axis)
    return swap(block, (axis,), lambda i: ((((i + 1) ^ 1) - 1) % count,))


def model_keep(wet_ref):
    wet = wet_ref[...].astype(F32)
    return jnp.where(lax.axis_index("grid") == 1, wet, jnp.ones_like(wet))


def pack_outer(rows_ref, packed_ref, lots, base=0):
    lane = lax.broadcasted_iota(jnp.int32, (16, LON), 1)
    outer = (lane < 3) | (lane >= LON - 3)
    for row in range(ROWS):
        for lot in range(lots):
            total = jnp.zeros((16, LON), F32)
            for block in range(16):
                start = (lot * 16 + block) * 16
                values = rows_ref[row, start : start + 16, :].astype(F32)
                values = jnp.where(outer, values, 0.0)
                total = total + (pltpu.roll(values, 8 * block, 1) if block else values)
            packed_ref[row, lot * 16 : lot * 16 + 16, :] = total.astype(BF)


def prepare_kernel(
    field_ref, wet_ref, rows_ref, even_ref, odd_ref, surface_ref, packed_ref, scratch
):
    chans = field_ref.shape[0]
    keep = model_keep(wet_ref)
    held = field_ref[...].astype(F32) * keep[None]
    scratch[...] = held.reshape(chans * ROWS, LON)
    for row in range(ROWS):
        rows_ref[row] = scratch[pl.ds(row, chans, stride=ROWS), :].astype(BF)
    parity = lax.rem(lax.axis_index("lat"), 2)

    @pl.when(parity == 0)
    def _():
        even_ref[...] = rows_ref[ROWS - 3 :]
        odd_ref[...] = rows_ref[:3]

    @pl.when(parity == 1)
    def _():
        even_ref[...] = rows_ref[:3]
        odd_ref[...] = rows_ref[ROWS - 3 :]

    @pl.when(pl.program_id(0) == 0)
    def _():
        surface_ref[...] = rows_ref[:, :KF, :]

    pack_outer(rows_ref, packed_ref, 1)


def prepare(field, wet_mask):
    stacked = field.shape[0]
    part = 256
    return pl.pallas_call(
        prepare_kernel,
        grid=(stacked // part,),
        in_specs=[
            pl.BlockSpec((part, ROWS, LON), lambda s: (s, 0, 0)),
            pl.BlockSpec((ROWS, LON), lambda s: (0, 0)),
        ],
        out_specs=[
            pl.BlockSpec((ROWS, part, LON), lambda s: (0, s, 0)),
            pl.BlockSpec((3, part, LON), lambda s: (0, s, 0)),
            pl.BlockSpec((3, part, LON), lambda s: (0, s, 0)),
            pl.BlockSpec((ROWS, KF, LON), lambda s: (0, 0, 0)),
            pl.BlockSpec((ROWS, 16, LON), lambda s: (0, s, 0)),
        ],
        out_shape=[
            jax.ShapeDtypeStruct((ROWS, stacked, LON), BF),
            jax.ShapeDtypeStruct((3, stacked, LON), BF),
            jax.ShapeDtypeStruct((3, stacked, LON), BF),
            jax.ShapeDtypeStruct((ROWS, KF, LON), BF),
            jax.ShapeDtypeStruct((ROWS, stacked // 16, LON), BF),
        ],
        scratch_shapes=[pltpu.VMEM((part * ROWS, LON), F32)],
        compiler_params=params(),
        cost_estimate=cost(10**6, 5 * 10**6),
        name="prepare",
    )(field, wet_mask)


def ready_kernel(models, row_ref, *refs):
    inputs, refs = refs[:6], refs[6:]
    in_t_ref, out_t_ref, bias_ref, table_ref, taps_ref = refs

    def run(first, chans, w_in, w_out, kernel):
        units = w_out.shape[0]
        in_t_ref[:units, :chans] = w_in[...].T
        out_t_ref[:chans, :units] = w_out[...].T

        def column(start):
            return jnp.broadcast_to(row_ref[0:1, start : start + LON], (LON, LON)).T

        for start in range(0, units, LON):
            bias_ref[start : start + LON, :] = column(first + start)
        for k in range(4):
            for start in range(0, chans, LON):
                table_ref[k, start : start + LON, :] = column(first + units + k * chans + start)
        taken = kernel.shape[0]
        tap = lax.broadcasted_iota(jnp.int32, (taken, LON), 0)
        group = lax.broadcasted_iota(jnp.int32, (taken, LON), 1) // 16
        by_chan = jnp.transpose(kernel[...]).astype(BF)
        for col in range(7):
            for flip in range(2):
                wanted = (6 - group) * 7 + (6 - col) if flip else group * 7 + col
                pick = ((tap == wanted) & (group < 7)).astype(F32).astype(BF)
                spread = jnp.dot(by_chan, pick, preferred_element_type=F32)
                taps_ref[flip, col, :chans, :] = spread.astype(BF)

    first = 0
    for which, (chans, _) in enumerate(models):
        w_in, w_out, kernel = inputs[3 * which : 3 * which + 3]

        @pl.when(lax.axis_index("grid") == which)
        def _():
            run(first, chans, w_in, w_out, kernel)

        first += w_out.shape[0] + 4 * chans


def ready(models, rows, arrays):
    most = max(chans for chans, _ in models)
    units = max(arrays[1].shape[0], arrays[4].shape[0])
    return pl.pallas_call(
        functools.partial(ready_kernel, models),
        in_specs=[VMEM] * 7,
        out_specs=[VMEM] * 5,
        out_shape=[
            jax.ShapeDtypeStruct((units, most), BF),
            jax.ShapeDtypeStruct((most, units), BF),
            jax.ShapeDtypeStruct((units, LON), F32),
            jax.ShapeDtypeStruct((4, most, LON), F32),
            jax.ShapeDtypeStruct((2, 7, most, LON), BF),
        ],
        compiler_params=params(),
        cost_estimate=cost(10**9, 10 * 10**6),
        name="ready",
    )(jnp.concatenate(rows)[None], *arrays)


def cotangent_kernel(cot_ref, wet_ref, scale_ref, out_ref, scratch):
    chans = cot_ref.shape[0]
    keep = model_keep(wet_ref)
    held = cot_ref[...].astype(F32) * keep[None]
    scratch[...] = held.reshape(chans * ROWS, LON)
    scale = jnp.concatenate(
        [
            jnp.broadcast_to(scale_ref[0, 0:1, start : start + LON], (LON, LON)).T
            for start in range(0, chans, LON)
        ],
        axis=0,
    )
    for row in range(ROWS):
        out_ref[row] = (scale * scratch[pl.ds(row, chans, stride=ROWS), :]).astype(BF)


def scaled_cotangent(cot, wet_mask, scale_rows):
    stacked = cot.shape[0]
    part = 256
    return pl.pallas_call(
        cotangent_kernel,
        grid=(stacked // part,),
        in_specs=[
            pl.BlockSpec((part, ROWS, LON), lambda s: (s, 0, 0)),
            pl.BlockSpec((ROWS, LON), lambda s: (0, 0)),
            pl.BlockSpec((1, 1, part), lambda s: (s, 0, 0)),
        ],
        out_specs=pl.BlockSpec((ROWS, part, LON), lambda s: (0, s, 0)),
        out_shape=jax.ShapeDtypeStruct((ROWS, stacked, LON), BF),
        scratch_shapes=[pltpu.VMEM((part * ROWS, LON), F32)],
        compiler_params=params(),
        cost_estimate=cost(10**6, 4 * 10**6),
        name="scaled_cotangent",
    )(cot, wet_mask, scale_rows.reshape(stacked // part, 1, part))


def build_taps(taps_ref, chan_start, band_ref, slot):
    lane = lax.broadcasted_iota(jnp.int32, (16, LON), 1)
    chan = lax.broadcasted_iota(jnp.int32, (16, LON), 0)
    for col in range(7):
        values = taps_ref[col, pl.ds(chan_start, 16), :].astype(F32)
        kept = jnp.where(lax.rem(lane, 16) == chan, values, 0.0)
        band_ref[slot, col * 16 : col * 16 + 16, :] = kept.astype(BF)


def convolve(rows_ref, halo_ref, outer_ref, band_ref, slot, starts):
    lane = lax.broadcasted_iota(jnp.int32, (16, LON), 1)
    inner = []
    beyond = []
    for start in starts:
        place = pl.ds(pl.multiple_of(start, 16), 16)
        index = start // 16
        lot = pl.ds(pl.multiple_of((index // 16) * 16, 16), 16)
        turn = lax.rem(LON - 8 * lax.rem(index, 16), LON)
        inner.append(
            [halo_ref[row, place, :] for row in range(3)]
            + [rows_ref[row, place, :] for row in range(ROWS)]
            + [halo_ref[row, place, :] for row in range(3, 6)]
        )
        beyond.append(
            [pltpu.roll(outer_ref[row, lot, :], turn, 1).astype(BF) for row in range(TALL)]
        )
    count = len(starts)
    blank = jnp.zeros((16, 2 * count * LON), BF)
    wide = [
        jnp.concatenate([side[row] for side in inner + beyond], axis=1) for row in range(TALL)
    ] + [blank]
    band = band_ref[slot]
    totals = [[] for _ in starts]
    for row in range(ROWS):
        spread = jnp.concatenate(wide[row : row + 8], axis=0)
        terms = jnp.dot(band, spread, preferred_element_type=F32)
        for level in range(count):
            total = None
            for col in range(7):
                shift = col - 3
                here = slice(col * 16, col * 16 + 16)
                piece = terms[here, level * LON : (level + 1) * LON]
                if shift:
                    other = terms[here, (count + level) * LON : (count + level + 1) * LON]
                    edge = lane < shift if shift > 0 else lane >= LON + shift
                    piece = pltpu.roll(jnp.where(edge, other, piece), (-shift) % LON, 1)
                total = piece if total is None else total + piece
            totals[level].append(total)
    return [jnp.concatenate(total, axis=0) for total in totals]


def convolve_all(chans, levels, taps_ref, rows_ref, halo_ref, outer_ref, band_ref, finish):
    count = chans // 16 // STEPS

    def step(index, carry):
        bases = [pl.multiple_of((index * count + block) * 16, 16) for block in range(count)]
        for block, base in enumerate(bases):
            build_taps(taps_ref, base, band_ref, block)
        for block, base in enumerate(bases):
            starts = [base + level * chans for level in range(levels)]
            for start, total in zip(
                starts, convolve(rows_ref, halo_ref, outer_ref, band_ref, block, starts)
            ):
                finish(start, total)
        return carry

    lax.fori_loop(0, STEPS, step, 0)


def merge_outer(outer_in, corner_even, corner_odd, outer_ref):
    first, top_live, bottom_live = lat_place()
    for row in range(3):
        even = corner_even[row].astype(F32)
        odd = corner_odd[row].astype(F32)
        outer_ref[row] = jnp.where(first, odd, even) * top_live
        outer_ref[ROWS + 3 + row] = jnp.where(first, even, odd) * bottom_live
    for row in range(ROWS):
        outer_ref[3 + row] = outer_in[row].astype(F32)


def lat_place():
    lat = lax.axis_index("lat")
    top = (lat > 0).astype(F32)
    bottom = (lat < lax.axis_size("lat") - 1).astype(F32)
    return lax.rem(lat, 2) == 0, top, bottom


def halo_copies(even_ref, odd_ref, halo_ref, sems):
    odd_lat = lax.rem(lax.axis_index("lat"), 2)
    return [
        pltpu.make_async_copy(even_ref, halo_ref.at[pl.ds(3 - 3 * odd_lat, 3)], sems.at[0]),
        pltpu.make_async_copy(odd_ref, halo_ref.at[pl.ds(3 * odd_lat, 3)], sems.at[1]),
    ]


def blank_beyond(halo_ref):
    lat = lax.axis_index("lat")

    @pl.when(lat == 0)
    def _():
        halo_ref[:3] = jnp.zeros_like(halo_ref[:3])

    @pl.when(lat == lax.axis_size("lat") - 1)
    def _():
        halo_ref[3:] = jnp.zeros_like(halo_ref[3:])


def adjoint_kernel(
    models,
    rows_hbm,
    even_hbm,
    odd_hbm,
    outer_in,
    corner_even,
    corner_odd,
    taps_hbm,
    cot_hbm,
    wet_ref,
    first_ref,
    out_ref,
    rows_ref,
    halo_ref,
    taps_ref,
    cot_ref,
    outer_ref,
    band_ref,
    sems,
):
    copies = [
        pltpu.make_async_copy(rows_hbm, rows_ref, sems.at[2]),
        pltpu.make_async_copy(taps_hbm.at[1], taps_ref, sems.at[3]),
        pltpu.make_async_copy(cot_hbm, cot_ref, sems.at[4]),
    ] + halo_copies(even_hbm, odd_hbm, halo_ref, sems)
    for copy in copies:
        copy.start()
    merge_outer(outer_in, corner_even, corner_odd, outer_ref)
    keep = model_keep(wet_ref)
    for copy in copies:
        copy.wait()
    blank_beyond(halo_ref)

    def finish(start, total):
        place = pl.ds(pl.multiple_of(start, 16), 16)
        by_chan = jnp.swapaxes(total.reshape(ROWS, 16, LON), 0, 1)
        whole = cot_ref[place].astype(F32) * keep[None] + by_chan
        out_ref[place] = (whole * keep[None]).astype(BF)
        first_ref[jnp.where(jnp.asarray(start == 0), 0, 1)] = whole

    for which, (chans, levels) in enumerate(models):

        @pl.when(lax.axis_index("grid") == which)
        def _():
            convolve_all(
                chans, levels, taps_ref, rows_ref, halo_ref, outer_ref, band_ref, finish
            )


def conv_scratch(stacked, most):
    return [
        pltpu.VMEM((ROWS, stacked, LON), BF),
        pltpu.VMEM((6, stacked, LON), BF),
        pltpu.VMEM((7, most, LON), BF),
    ]


def adjoint(models, rows, even, odd, outer, corner_even, corner_odd, taps, cot, wet_mask):
    stacked = rows.shape[1]
    most = taps.shape[2]
    return pl.pallas_call(
        functools.partial(adjoint_kernel, models),
        in_specs=[ANY] * 3 + [VMEM] * 3 + [ANY] * 2 + [VMEM],
        out_specs=[VMEM, VMEM],
        out_shape=[
            jax.ShapeDtypeStruct((2, KF, ROWS, LON), F32),
            jax.ShapeDtypeStruct((stacked, ROWS, LON), BF),
        ],
        scratch_shapes=conv_scratch(stacked, most)
        + [
            pltpu.VMEM((stacked, ROWS, LON), BF),
            pltpu.VMEM((TALL, stacked // 16, LON), F32),
            pltpu.VMEM((3, 112, LON), BF),
            pltpu.SemaphoreType.DMA((5,)),
        ],
        compiler_params=params(),
        cost_estimate=cost(3 * 10**9, 8 * 10**6),
        name="adjoint",
    )(rows, even, odd, outer, corner_even, corner_odd, taps, cot, wet_mask)


def couple_kernel(first_ref, near_ref, far_ref, wet_ref, _, out_hbm, held_ref, sem):
    both = near_ref[...].astype(F32) + far_ref[...].astype(F32)
    keep = model_keep(wet_ref)
    held_ref[...] = ((first_ref[0] + jnp.swapaxes(both, 0, 1)) * keep[None]).astype(BF)
    copy = pltpu.make_async_copy(held_ref, out_hbm.at[pl.ds(0, KF)], sem)
    copy.start()
    copy.wait()


def couple(first, near, far, wet_mask, grads):
    return pl.pallas_call(
        couple_kernel,
        in_specs=[VMEM] * 4 + [ANY],
        out_specs=ANY,
        out_shape=jax.ShapeDtypeStruct(grads.shape, BF),
        input_output_aliases={4: 0},
        scratch_shapes=[pltpu.VMEM((KF, ROWS, LON), BF), pltpu.SemaphoreType.DMA],
        compiler_params=params(),
        cost_estimate=cost(10**5, 10**6),
        name="couple",
    )(first, near, far, wet_mask, grads)


def advance_kernel(rows_ref, wet_ref, out_ref):
    keep = model_keep(wet_ref)

    def turn(index, carry):
        place = pl.ds(pl.multiple_of(index * 16, 16), 16)
        by_chan = jnp.swapaxes(rows_ref[:, place, :].astype(F32), 0, 1)
        out_ref[place] = (by_chan * keep[None]).astype(BF)
        return carry

    lax.fori_loop(0, rows_ref.shape[1] // 16, turn, 0)


def advance(rows, wet_mask):
    stacked = rows.shape[1]
    part = 256
    return pl.pallas_call(
        advance_kernel,
        grid=(stacked // part,),
        in_specs=[
            pl.BlockSpec((ROWS, part, LON), lambda s: (0, s, 0)),
            pl.BlockSpec((ROWS, LON), lambda s: (0, 0)),
        ],
        out_specs=pl.BlockSpec((part, ROWS, LON), lambda s: (s, 0, 0)),
        out_shape=jax.ShapeDtypeStruct((stacked, ROWS, LON), BF),
        compiler_params=params(),
        cost_estimate=cost(10**6, 4 * 10**6),
        name="advance",
    )(rows, wet_mask)


def slot_of(source):
    apart = source ^ lax.axis_index("lon")
    far = apart >> 2
    return far | ((((apart >> 1) ^ far) & 1) << 1) | (((apart ^ far) & 1) << 2)


def cells_kernel(models, *refs):
    (
        rows_hbm,
        even_hbm,
        odd_hbm,
        outer_in,
        corner_even,
        corner_odd,
        taps_hbm,
        up_hbm,
        wet_ref,
        sources_ref,
        regrid_hbm,
        *refs,
    ) = refs
    pieces_hbm, refs = refs[:4], refs[4:]
    weights, refs = refs[:8], refs[8:]
    (advanced_hbm, grad_hbm, even_out, odd_out, packed_ref, *terms), refs = refs[:7], refs[7:]
    rows_ref, halo_ref, taps_ref, up_ref, regrid_ref, pieces_ref, outer_ref, band_ref = refs[:8]
    mixed_ref, forcing_ref, advanced_ref, grad_ref = refs[8:12]
    kept, refs = (refs[12:16], refs[16:20]), refs[20:]
    in_t_v, out_n_v, out_t_v, in_n_v, bias_v, table_v, sems, weight_sems = refs
    early = halo_copies(even_hbm, odd_hbm, halo_ref, sems) + [
        pltpu.make_async_copy(rows_hbm, rows_ref, sems.at[2]),
        pltpu.make_async_copy(taps_hbm.at[0], taps_ref, sems.at[3]),
    ]
    late = [
        pltpu.make_async_copy(src, dst, sems.at[4 + k])
        for k, (src, dst) in enumerate(
            [(up_hbm, up_ref), (regrid_hbm, regrid_ref)]
            + [
                (piece, pieces_ref.at[pl.ds(start, piece.shape[0])])
                for piece, start in zip(pieces_hbm, (0, 1, 2, 4))
            ]
        )
    ]
    for copy in early:
        copy.start()
    for copy in late:
        copy.start()
    merge_outer(outer_in, corner_even, corner_odd, outer_ref)
    for copy in early:
        copy.wait()
    blank_beyond(halo_ref)

    def mix(chans, levels):
        def finish(start, total):
            place = pl.ds(pl.multiple_of(start, 16), 16)
            for row in range(ROWS):
                mixed_ref[row, place, :] = total[row * 16 : row * 16 + 16]

        convolve_all(chans, levels, taps_ref, rows_ref, halo_ref, outer_ref, band_ref, finish)

    def force():
        for copy in late:
            copy.wait()
        slots = [slot_of(sources_ref[0, p]) for p in range(3)]
        for row in range(ROWS):
            total = None
            for p in range(3):
                part = lax.dot_general(
                    pieces_ref[slots[p], row],
                    regrid_ref[p, row],
                    (((1,), (1,)), ((), ())),
                    preferred_element_type=F32,
                )
                total = part if total is None else total + part
            forcing_ref[row] = total
        for ref in terms:
            ref[...] = jnp.zeros_like(ref)
        return slots

    def run(which, chans, levels):
        in_t, out_t, bias, table = weights[4:]
        in_n, out_n = weights[2 * which : 2 * which + 2]
        hidden_units = out_n.shape[0]
        units, wide_chans = pl.ds(0, hidden_units), pl.ds(0, chans)
        in_t_w, out_n_w = in_t_v.at[units, wide_chans], out_n_v.at[units, wide_chans]
        out_t_w, in_n_w = out_t_v.at[wide_chans, units], in_n_v.at[wide_chans, units]
        copies = [
            pltpu.make_async_copy(src, dst, weight_sems.at[k])
            for k, (src, dst) in enumerate(
                (
                    (in_t.at[units, wide_chans], in_t_w),
                    (out_n, out_n_w),
                    (out_t.at[wide_chans, units], out_t_w),
                    (in_n, in_n_w),
                    (bias, bias_v),
                    (table, table_v),
                )
            )
        ]
        for copy in copies:
            copy.start()
        gain_v, shift_v, bias_out_v, scale_v = [table_v.at[k, wide_chans] for k in range(4)]
        mix(chans, levels)
        slots = force()
        for copy in copies:
            copy.wait()
        share = 1.0 / chans
        wide = 2 * LON
        part = 256

        def pair(values):
            return jnp.concatenate([values, values], axis=1)

        def place_of(index):
            return lax.rem(index, 4) * 2, pl.ds(pl.multiple_of(index // 4 * chans, 16), chans)

        def front(index, slot):
            row, place = place_of(index)
            live = jnp.asarray(index < 4).astype(F32)
            act_ref, back_ref, unit_ref, inverse_ref = kept[slot]
            normed = []
            for k in range(2):
                mixed = mixed_ref[row + k, place, :]
                top = mixed[:KF] + forcing_ref[row + k] * live
                mixed = jnp.concatenate([top, mixed[KF:]], axis=0)
                centre = jnp.sum(mixed, axis=0, keepdims=True) * share
                spread = mixed - centre
                inverse = lax.rsqrt(jnp.sum(spread * spread, axis=0, keepdims=True) * share + EPS)
                unit = spread * inverse
                unit_ref[k, :chans, :] = unit
                inverse_ref[k] = jnp.broadcast_to(inverse, (8, LON))
                normed.append((unit * gain_v[...] + shift_v[...]).astype(BF))
            normed = jnp.concatenate(normed, axis=1)
            up = jnp.concatenate([up_ref[row, place, :], up_ref[row + 1, place, :]], axis=1)
            for start in range(0, hidden_units, part):
                these = slice(start, start + part)
                hidden = jnp.dot(in_t_w[these, :], normed, preferred_element_type=F32)
                active_grad = jnp.dot(out_n_w[these, :], up, preferred_element_type=F32)
                hidden = hidden + pair(bias_v[these, :])
                below = 0.5 + 0.5 * lax.erf(hidden * INV_ROOT_TWO)
                act_ref[these, :] = (hidden * below).astype(BF)
                bell = jnp.exp2((hidden * hidden) * -HALF_LOG2E) * NORMAL_PEAK
                back_ref[these, :] = (active_grad * (below + hidden * bell)).astype(BF)

        def back(index, slot):
            row, place = place_of(index)
            act_ref, back_ref, unit_ref, inverse_ref = kept[slot]
            update = jnp.dot(
                out_t_w[...], act_ref[:hidden_units, :], preferred_element_type=F32
            )
            normed_grad = jnp.dot(
                in_n_w[...], back_ref[:hidden_units, :], preferred_element_type=F32
            )
            for k in range(2):
                lanes = slice(k * LON, (k + 1) * LON)
                moved = scale_v[...] * (update[:, lanes] + bias_out_v[...])
                total = rows_ref[row + k, place, :].astype(F32) + moved
                advanced_ref[row + k, place, :] = total.astype(BF)
                scaled = normed_grad[:, lanes] * gain_v[...]
                unit = unit_ref[k, :chans, :]
                mean = jnp.sum(scaled, axis=0, keepdims=True) * share
                slope = jnp.sum(scaled * unit, axis=0, keepdims=True) * share
                inverse = inverse_ref[k, 0:1, :]
                grad_ref[row + k, place, :] = (inverse * (scaled - mean - unit * slope)).astype(BF)

        count = levels * 4
        front(0, 0)

        def turn(index, carry):
            front(2 * index + 1, 1)
            back(2 * index, 0)
            front(2 * index + 2, 0)
            back(2 * index + 1, 1)
            return carry

        lax.fori_loop(0, count // 2 - 1, turn, 0)
        front(count - 1, 1)
        back(count - 2, 0)
        back(count - 1, 1)
        for row in range(ROWS):
            for p in range(3):
                term = jnp.dot(
                    grad_ref[row, :KF, :], regrid_ref[p, row], preferred_element_type=F32
                ).astype(BF)
                for side, ref in enumerate(terms):

                    @pl.when(slots[p] // 4 == side)
                    def _():
                        ref[lax.rem(slots[p], 4), row] = term

    for which, (chans, levels) in enumerate(models):

        @pl.when(lax.axis_index("grid") == which)
        def _():
            run(which, chans, levels)

    odd_lat = lax.rem(lax.axis_index("lat"), 2)
    lower = ROWS - 3
    leaving = [
        pltpu.make_async_copy(grad_ref.at[pl.ds(lower * (1 - odd_lat), 3)], even_out, sems.at[0]),
        pltpu.make_async_copy(grad_ref.at[pl.ds(lower * odd_lat, 3)], odd_out, sems.at[1]),
        pltpu.make_async_copy(grad_ref, grad_hbm, sems.at[2]),
        pltpu.make_async_copy(advanced_ref, advanced_hbm, sems.at[3]),
    ]
    for copy in leaving:
        copy.start()
    pack_outer(grad_ref, packed_ref, grad_ref.shape[1] // 256)
    for copy in leaving:
        copy.wait()


def cells(
    models,
    rows,
    even,
    odd,
    outer,
    corner_even,
    corner_odd,
    taps,
    up,
    wet_mask,
    sources,
    regrid,
    pieces,
    weights,
):
    stacked = rows.shape[1]
    most_chans = max(chans for chans, _ in models)
    most_units = weights[4].shape[0]
    return pl.pallas_call(
        functools.partial(cells_kernel, models),
        in_specs=[ANY] * 3
        + [VMEM] * 3
        + [ANY] * 2
        + [VMEM, SMEM]
        + [ANY] * (1 + 4 + 8),
        out_specs=[ANY] * 4 + [VMEM] * 3,
        out_shape=[
            jax.ShapeDtypeStruct((ROWS, stacked, LON), BF),
            jax.ShapeDtypeStruct((ROWS, stacked, LON), BF),
            jax.ShapeDtypeStruct((3, stacked, LON), BF),
            jax.ShapeDtypeStruct((3, stacked, LON), BF),
            jax.ShapeDtypeStruct((ROWS, stacked // 16, LON), BF),
            jax.ShapeDtypeStruct((4, ROWS, KF, LON), BF),
            jax.ShapeDtypeStruct((4, ROWS, KF, LON), BF),
        ],
        scratch_shapes=conv_scratch(stacked, taps.shape[2])
        + [
            pltpu.VMEM(up.shape, BF),
            pltpu.VMEM(regrid.shape, BF),
            pltpu.VMEM((8, ROWS, KF, LON), BF),
            pltpu.VMEM((TALL, stacked // 16, LON), F32),
            pltpu.VMEM((3, 112, LON), BF),
            pltpu.VMEM((ROWS, stacked, LON), F32),
            pltpu.VMEM((ROWS, KF, LON), F32),
            pltpu.VMEM((ROWS, stacked, LON), BF),
            pltpu.VMEM((ROWS, stacked, LON), BF),
        ]
        + [
            pltpu.VMEM((most_units, 2 * LON), BF),
            pltpu.VMEM((most_units, 2 * LON), BF),
            pltpu.VMEM((2, most_chans, LON), F32),
            pltpu.VMEM((2, 8, LON), F32),
        ]
        * 2
        + [
            pltpu.VMEM((most_units, most_chans), BF),
            pltpu.VMEM((most_units, most_chans), BF),
            pltpu.VMEM((most_chans, most_units), BF),
            pltpu.VMEM((most_chans, most_units), BF),
            pltpu.VMEM((most_units, LON), F32),
            pltpu.VMEM((4, most_chans, LON), F32),
            pltpu.SemaphoreType.DMA((10,)),
            pltpu.SemaphoreType.DMA((6,)),
        ],
        compiler_params=params(),
        cost_estimate=cost(10**10, 20 * 10**6),
        name="cells",
    )(
        rows,
        even,
        odd,
        outer,
        corner_even,
        corner_odd,
        taps,
        up,
        wet_mask,
        sources,
        regrid,
        *pieces,
        *weights,
    )


def east_west(packed, even, odd):
    first = lax.rem(lax.axis_index("lon"), 2) == 0
    lane = lax.broadcasted_iota(jnp.int32, packed.shape, 2)
    return jnp.where((lax.rem(lane, 8) < 4) == first, even, odd)


def facing(packed):
    north = lax.rem(lax.axis_index("lat"), 2) == 1
    ends = (packed[:3], packed[ROWS - 3 :])
    return jnp.where(north, ends[0], ends[1]), jnp.where(north, ends[1], ends[0])


def swap_outer(packed):
    outer = east_west(packed, even_swap(packed, "lon"), odd_swap(packed, "lon"))
    even, odd = facing(outer)
    return outer, even_swap(even, "lat"), odd_swap(odd, "lat")


def cross(block, apart):
    return swap(block, ("grid", "lon"), lambda g, j: (1 - g, j ^ apart))


def lon_swap(block, apart):
    return swap(block, ("lon",), lambda j: (j ^ apart,))


def per_device(
    fields,
    cotangent,
    wet_mask,
    atmos_kernel,
    atmos_gain,
    atmos_shift,
    atmos_w_in,
    atmos_b_in,
    atmos_w_out,
    atmos_b_out,
    atmos_scale,
    ocean_kernel,
    ocean_gain,
    ocean_shift,
    ocean_w_in,
    ocean_b_in,
    ocean_w_out,
    ocean_b_out,
    ocean_scale,
    sources,
    regrid,
):
    stacked = fields.shape[1]
    models = tuple((w.shape[0], stacked // w.shape[0]) for w in (atmos_w_in, ocean_w_in))
    is_ocean = lax.axis_index("grid") == 1
    field, cot = fields[0], cotangent[0]
    rows, even, odd, surface, packed = prepare(field, wet_mask)
    pieces = [cross(surface[None], 0), cross(surface[None], 7)]
    around = swap_outer(packed)
    even = even_swap(even, "lat")
    odd = odd_swap(odd, "lat")
    scale_rows = jnp.where(
        is_ocean,
        jnp.tile(ocean_scale, models[1][1]),
        jnp.tile(atmos_scale, models[0][1]),
    )
    joined, wet_then = lax.optimization_barrier((jnp.concatenate(pieces, axis=0), wet_mask))
    pieces.append(lon_swap(joined, 2))
    up = scaled_cotangent(cot, wet_then, scale_rows)
    *pieces, up = lax.optimization_barrier((*pieces, up))
    pieces.append(lon_swap(jnp.concatenate(pieces, axis=0), 1))
    made = ready(
        models,
        (
            atmos_b_in,
            atmos_gain,
            atmos_shift,
            atmos_b_out,
            atmos_scale,
            ocean_b_in,
            ocean_gain,
            ocean_shift,
            ocean_b_out,
            ocean_scale,
        ),
        (
            atmos_w_in,
            atmos_w_out,
            atmos_kernel.T,
            ocean_w_in,
            ocean_w_out,
            ocean_kernel.T,
        ),
    )
    around, pieces, made = lax.optimization_barrier((around, pieces, made))
    in_t, out_t, bias, table, taps = made
    weights = [atmos_w_in, atmos_w_out, ocean_w_in, ocean_w_out, in_t, out_t, bias, table]
    advanced, grad, even, odd, packed, near, far = cells(
        models,
        rows,
        even,
        odd,
        *around,
        taps,
        up,
        wet_mask,
        sources[0, 0],
        regrid[0, 0, 0],
        pieces,
        weights,
    )
    came = lon_swap(far, 1)
    outer = east_west(packed, even_swap(packed, "lon"), odd_swap(packed, "lon"))
    even = even_swap(even, "lat")
    odd = odd_swap(odd, "lat")
    sums = [(near[k : k + 2].astype(F32) + came[k : k + 2].astype(F32)) for k in (0, 2)]
    lot, *corners, wet_then = lax.optimization_barrier(
        (sums[1].astype(BF), *facing(outer), wet_mask)
    )
    came = lon_swap(lot, 2)
    around = (outer, even_swap(corners[0], "lat"), odd_swap(corners[1], "lat"))
    advanced = advance(advanced, wet_then)
    came, advanced = lax.optimization_barrier((came, advanced))
    ends = [(sums[0][k] + came[k].astype(F32)).astype(BF) for k in range(2)]
    coupling = cross(ends[0], 0), cross(ends[1], 7)
    first, field_grads = adjoint(models, grad, even, odd, *around, taps, cot, wet_mask)
    field_grads = couple(first, *coupling, wet_mask, field_grads)
    return (advanced[None], field_grads[None])


def solution(mesh):
    placed = (
        (P("grid", None, "lat", "lon"),) * 2
        + (P("lat", "lon"),)
        + (P(),) * 16
        + (P("grid", "lat", "lon", None), P("grid", "lat", "lon", None, None, None, None))
    )
    return jax.shard_map(
        per_device,
        mesh=mesh,
        in_specs=placed,
        out_specs=(P("grid", None, "lat", "lon"), P("grid", None, "lat", "lon")),
        check_vma=False,
    )
```
